256 devices in a mesh: space: 64 (over x, z, core), chan: 4 (over y).
Axes of the slice: x: 4, y: 4, z: 8, core: 2. Of those that a mesh axis runs over, the one named last changes fastest.
Arguments:
- features: bfloat16 [128, 256, 512], P('chan', 'space'), may hold values from -6 to 6
- weight: bfloat16 [27, 128, 128], P(None, 'chan'), may hold values from -0.21875 to 0.21875
- cotangent: bfloat16 [128, 256, 512], P('chan', 'space'), may hold values from -6 to 6
- neighbours: int32 [256, 27], P('space'), may hold values from 0 to 68, as said below
- send_slots: int32 [512, 8], P('space'), may hold values from 0 to 4, as said below
Outputs:
- output: bfloat16 [128, 256, 512], P('chan', 'space')
- grad_input: bfloat16 [128, 256, 512], P('chan', 'space')
- grad_weight: float32 [27, 128, 128], P(None, 'chan')
The draws below stay inside these ranges and needn't reach their ends.
Inputs may be any that keep to these rules, and one draw needn't show every extreme that they name: `neighbours`: each owner has a tile of 4 x 4 x 2 brick places; its occupied places fill its first brick slots, and in some owner all 4 slots are occupied. Row b, column 9 (ox + 1) + 3 (oy + 1) + oz + 1 names the pool entry of the brick at brick offset (ox, oy, oz) from brick b, 0 where that place is empty or outside the grid; rows of unoccupied slots are all 0. Between occupied bricks the relation is symmetric: if b2 is at offset (ox, oy, oz) from b, b is at (-ox, -oy, -oz) from b2. Entries 1 + d * 8 + j occur only where the owner in direction d exists and lists an occupied brick in slot j of its side facing back. `send_slots`: row 8 s + e lists, one slot per brick place in a fixed order, the bricks of owner s on its tile's side facing direction e: a face of 4 x 2 or 4 x 2 places, or a corner column of 2 places; 4 marks an empty place, an unused slot, or a side whose neighbouring owner does not exist.
All inputs are finite; a program needn't handle non-finite values.
Results may differ from the reference program's by a relative error of at most 0.0042.
Values may be sent and summed in bfloat16 or wider, within the bound.
No kernel may reach another device: no remote copies, remote signals or barrier semaphores. Data moves between devices by JAX's collectives and lax.ppermute only.
A program may use at most 192 MiB of HBM per device.

```python
import jax
import jax.numpy as jnp
from jax import lax

CHANNELS = 128
BRICK_DEV = 4
TILE_X = 4
TILE_Y = 4
TILE_Z = 2
OWNER_ROWS = 4
VOXELS = 512
TAPS = 27
SLOTS = 8
BRICKS = 256
N_SPACE = 64


compass = ((-1, -1), (-1, 0), (-1, 1), (0, -1), (0, 1), (1, -1), (1, 0), (1, 1))


def city_layout(key):
    cell_total = TILE_X * TILE_Y * TILE_Z
    key_count, key_busy, key_score = jax.random.split(key, 3)
    owners = jnp.arange(N_SPACE, dtype=jnp.int32)
    filled = jax.random.randint(key_count, (N_SPACE,), max(1, 3 * BRICK_DEV // 4), BRICK_DEV + 1)
    busiest = jax.random.randint(key_busy, (), 0, N_SPACE)
    filled = jnp.where(owners == busiest, BRICK_DEV, filled)
    cell_ids = jnp.arange(cell_total, dtype=jnp.int32)
    scores = jax.random.randint(key_score, (N_SPACE, cell_total), 0, 2 ** 20) * cell_total + cell_ids[None, :]
    scores = scores.at[:, 0].set(2 ** 30)
    order = jnp.argsort(-scores, axis=1)
    ranking = jnp.argsort(order, axis=1)
    occupied = ranking < filled[:, None]
    local_ids = jnp.cumsum(occupied.astype(jnp.int32), axis=1) - 1
    cell_x = cell_ids // (TILE_Y * TILE_Z)
    cell_y = cell_ids // TILE_Z % TILE_Y
    cell_z = cell_ids % TILE_Z
    tile_x = owners // OWNER_ROWS
    tile_y = owners % OWNER_ROWS
    tiles_x = N_SPACE // OWNER_ROWS
    taps = jnp.arange(27, dtype=jnp.int32)
    target_x = cell_x[None, :, None] + (taps // 9 - 1)[None, None, :]
    target_y = cell_y[None, :, None] + (taps // 3 % 3 - 1)[None, None, :]
    target_z = cell_z[None, :, None] + (taps % 3 - 1)[None, None, :]
    step_x = jnp.where(target_x < 0, -1, jnp.where(target_x >= TILE_X, 1, 0))
    step_y = jnp.where(target_y < 0, -1, jnp.where(target_y >= TILE_Y, 1, 0))
    inner_x = target_x - step_x * TILE_X
    inner_y = target_y - step_y * TILE_Y
    peer_x = tile_x[:, None, None] + step_x
    peer_y = tile_y[:, None, None] + step_y
    tile_ok = (peer_x >= 0) & (peer_x < tiles_x) & (peer_y >= 0) & (peer_y < OWNER_ROWS)
    z_ok = (target_z >= 0) & (target_z < TILE_Z)
    inner_z = jnp.clip(target_z, 0, TILE_Z - 1)
    peer = jnp.clip(peer_x * OWNER_ROWS + peer_y, 0, N_SPACE - 1)
    peer_cell = jnp.clip(inner_x * TILE_Y * TILE_Z + inner_y * TILE_Z + inner_z, 0, cell_total - 1)
    peer_occupied = occupied[peer, peer_cell]
    peer_ids = local_ids[peer, peer_cell]
    compass_code = (step_x + 1) * 3 + (step_y + 1)
    direction = jnp.where(compass_code > 4, compass_code - 1, compass_code)
    slot_index = jnp.where(step_y == 0, inner_y * TILE_Z + inner_z, jnp.where(step_x == 0, inner_x * TILE_Z + inner_z, inner_z))
    at_home = (step_x == 0) & (step_y == 0)
    pool_index = jnp.where(at_home, 1 + 8 * SLOTS + peer_ids, 1 + direction * SLOTS + slot_index)
    valid = z_ok & tile_ok & peer_occupied
    values = jnp.where(valid, pool_index, 0).astype(jnp.int32)
    row_place = jnp.where(occupied, local_ids, BRICK_DEV)
    lookup = jnp.zeros((N_SPACE, BRICK_DEV, 27), jnp.int32)
    lookup = lookup.at[owners[:, None, None], row_place[:, :, None], taps[None, None, :]].set(values, mode='drop')
    slot_ids = jnp.arange(SLOTS, dtype=jnp.int32)
    side_rows = []
    for facing in compass:
        if facing[0] != 0 and facing[1] != 0:
            side_x = slot_ids * 0 + (TILE_X - 1 if facing[0] > 0 else 0)
            side_y = slot_ids * 0 + (TILE_Y - 1 if facing[1] > 0 else 0)
            side_z = slot_ids
            slot_ok = slot_ids < TILE_Z
        elif facing[0] != 0:
            side_x = slot_ids * 0 + (TILE_X - 1 if facing[0] > 0 else 0)
            side_y = slot_ids // TILE_Z
            side_z = slot_ids % TILE_Z
            slot_ok = slot_ids < TILE_Y * TILE_Z
        else:
            side_y = slot_ids * 0 + (TILE_Y - 1 if facing[1] > 0 else 0)
            side_x = slot_ids // TILE_Z
            side_z = slot_ids % TILE_Z
            slot_ok = slot_ids < TILE_X * TILE_Z
        side_cell = jnp.clip(side_x * TILE_Y * TILE_Z + side_y * TILE_Z + side_z, 0, cell_total - 1)
        target_ok = (tile_x + facing[0] >= 0) & (tile_x + facing[0] < tiles_x) & (tile_y + facing[1] >= 0) & (tile_y + facing[1] < OWNER_ROWS)
        keep = slot_ok[None, :] & occupied[:, side_cell] & target_ok[:, None]
        side_rows.append(jnp.where(keep, local_ids[:, side_cell], BRICK_DEV).astype(jnp.int32))
    send_table = jnp.stack(side_rows, axis=1)
    return (lookup.reshape(N_SPACE * BRICK_DEV, 27), send_table.reshape(N_SPACE * 8, SLOTS))


def draw_neighbours(key, part):
    layout = city_layout(key)
    return layout[0]


def draw_send_slots(key, part):
    layout = city_layout(key)
    return layout[1]


def level_of(own_key, dims, cuts, low, top_value):
    def one(position, blocks):
        steps = jax.random.uniform(jax.random.fold_in(jax.random.fold_in(own_key, 6), position), (blocks,), jnp.float32, low / len(cuts), top_value / len(cuts))
        return jnp.repeat(jnp.exp(steps), dims[position] // blocks).reshape((-1,) + (1,) * (len(dims) - position - 1))

    level = one(*cuts[0])
    for cut in cuts[1:]:
        level = level * one(*cut)
    return level


def noise(rng, extent, deviation, reach, pieces=(), held_as=jnp.bfloat16):
    gain = level_of(rng, extent, pieces, -0.22, 0.18) if pieces else 1.0
    values = jax.random.normal(rng, extent, jnp.float32) * deviation * gain
    return jnp.minimum(jnp.maximum(values, -reach), reach).astype(held_as)


def setup_inputs(seed: int = 0) -> dict:
    key_of = jax.random.split(jax.random.key(seed), 6)
    return {
        "features": noise(key_of[0], (CHANNELS, BRICKS, VOXELS), 1.0, 6.0, ((0, 4), (1, 64))),
        "weight": noise(key_of[1], (TAPS, CHANNELS, CHANNELS), (TAPS * CHANNELS // 4) ** -0.5, 0.21875, ((1, 4),)),
        "cotangent": noise(key_of[2], (CHANNELS, BRICKS, VOXELS), 1.0, 6.0, ((0, 4), (1, 64))),
        "neighbours": draw_neighbours(jax.random.fold_in(key_of[5], 71), 0),
        "send_slots": draw_send_slots(jax.random.fold_in(key_of[5], 71), 0),
    }


def global_lookup(neighbours, send_slots):
    slot_count = send_slots.shape[1]
    send_table = send_slots.reshape(N_SPACE, 8, slot_count)
    entries = neighbours.reshape(N_SPACE, BRICK_DEV, 27)
    owners = jnp.arange(N_SPACE, dtype=jnp.int32)[:, None, None]
    remote = jnp.clip(entries - 1, 0, 8 * slot_count - 1)
    direction = remote // slot_count
    slot_index = remote % slot_count
    compass_code = jnp.where(direction >= 4, direction + 1, direction)
    step_x = compass_code // 3 - 1
    step_y = compass_code % 3 - 1
    source = jnp.clip(owners + step_x * OWNER_ROWS + step_y, 0, N_SPACE - 1)
    local_id = send_table[source, 7 - direction, slot_index]
    blank_row = N_SPACE * BRICK_DEV
    from_peer = jnp.where(local_id < BRICK_DEV, source * BRICK_DEV + local_id, blank_row)
    from_self = owners * BRICK_DEV + jnp.clip(entries - 1 - 8 * slot_count, 0, BRICK_DEV - 1)
    lookup = jnp.where(entries == 0, blank_row, jnp.where(entries <= 8 * slot_count, from_peer, from_self))
    return lookup.astype(jnp.int32)


def brick_margin(brick_pool, lookup):
    channels = brick_pool.shape[0]
    voxel_cube = brick_pool.reshape(channels, brick_pool.shape[1], 8, 8, 8)
    layer_cuts = ((7, 8), (0, 8), (0, 1))
    planes = []
    for i in range(3):
        x_slab = voxel_cube[:, :, layer_cuts[i][0]:layer_cuts[i][1]]
        row_parts = []
        for j in range(3):
            xy_slab = x_slab[:, :, :, layer_cuts[j][0]:layer_cuts[j][1]]
            column_parts = []
            for k in range(3):
                portion = xy_slab[:, :, :, :, layer_cuts[k][0]:layer_cuts[k][1]]
                column_parts.append(jnp.take(portion, lookup[:, 9 * i + 3 * j + k], axis=1))
            row_parts.append(jnp.concatenate(column_parts, axis=4))
        planes.append(jnp.concatenate(row_parts, axis=3))
    return jnp.concatenate(planes, axis=2)


def stack_group(padded, offset_x):
    channels, bricks = padded.shape[0], padded.shape[1]
    slices = []
    for j in range(3):
        for k in range(3):
            slices.append(padded[:, :, offset_x:offset_x + 8, j:j + 8, k:k + 8].reshape(channels, bricks * 512))
    return jnp.concatenate(slices, axis=0)


def convolve(stacks, weight):
    channels, all_chan = weight.shape[1], weight.shape[2]
    running = None
    for i in range(3):
        grouped = weight[9 * i:9 * i + 9].reshape(9 * channels, all_chan)
        term = jnp.dot(grouped.T, stacks[i], preferred_element_type=jnp.float32)
        running = term if i == 0 else running + term
    return running


def to_blocks(field):
    channels = field.shape[0]
    return field.reshape(channels, N_SPACE, BRICK_DEV * VOXELS).transpose(1, 0, 2)


def to_field(blocks):
    channels = blocks.shape[1]
    return blocks.transpose(1, 0, 2).reshape(channels, N_SPACE * BRICK_DEV, VOXELS)


def reference(features, weight, cotangent, neighbours, send_slots):
    lookup = global_lookup(neighbours, send_slots)
    channels = features.shape[0]
    blank = jnp.zeros((channels, 1, VOXELS), jnp.bfloat16)
    feat_ext = jnp.concatenate([features, blank], axis=1)
    feat_blocks = to_blocks(features)
    cot_blocks = to_blocks(cotangent)

    def forward(inputs):
        rows_now, feat_block, cot_block = inputs
        padded = brick_margin(feat_ext, rows_now)
        stacks = [stack_group(padded, i) for i in range(3)]
        hidden = convolve(stacks, weight)
        gate_sig = jax.nn.sigmoid(hidden)
        result = (feat_block.astype(jnp.float32) + hidden * gate_sig).astype(jnp.bfloat16)
        grad_h = (cot_block.astype(jnp.float32) * gate_sig * (1.0 + hidden * (1.0 - gate_sig))).astype(jnp.bfloat16)
        return result, grad_h

    out_blocks, grad_blocks = lax.map(forward, (lookup, feat_blocks, cot_blocks))
    grad_field = to_field(grad_blocks)
    grad_ext = jnp.concatenate([grad_field, blank], axis=1)
    flipped = jnp.flip(weight, 0).transpose(0, 2, 1)

    def backward(running, inputs):
        rows_now, grad_block, cot_block = inputs
        feat_stacks = [stack_group(brick_margin(feat_ext, rows_now), i) for i in range(3)]
        grad_stacks = [stack_group(brick_margin(grad_ext, rows_now), i) for i in range(3)]
        transposed = convolve(grad_stacks, flipped)
        grad_in = (cot_block.astype(jnp.float32) + transposed).astype(jnp.bfloat16)
        blocks = [jnp.dot(tap_stack, grad_block.T, preferred_element_type=jnp.float32).reshape(9, channels, channels) for tap_stack in feat_stacks]
        return running + jnp.concatenate(blocks, axis=0), grad_in

    start_value = jnp.zeros((TAPS, channels, channels), jnp.float32)
    grad_weight, input_blocks = lax.scan(backward, start_value, (lookup, grad_blocks, cot_blocks))
    return to_field(out_blocks), to_field(input_blocks), grad_weight
```

```python
import jax
import jax.numpy as jnp
from jax import lax
from jax.experimental import pallas as pl
from jax.experimental.pallas import tpu as pltpu
from jax.sharding import Mesh, PartitionSpec as P

ROWS = 4
CH = 128
BR = 4
VOX = 512
TAPS = 27
SLOTS = 8
ZERO = 36
F32 = jnp.float32
BF16 = jnp.bfloat16
SPACE = ("x", "z", "core")
XC = ("x", "core")
VMEM = pl.BlockSpec(memory_space=pltpu.VMEM)
SMEM = pl.BlockSpec(memory_space=pltpu.SMEM)

compass = ((-1, -1), (-1, 0), (-1, 1), (0, -1), (0, 1), (1, -1), (1, 0), (1, 1))
BASE = {facing: 4 + 4 * i for i, facing in enumerate(compass)}
PARAMS = pltpu.CompilerParams(vmem_limit_bytes=56 * 2**20)


def shifted(value, steps):
    count = lax.axis_size(SPACE)
    first, last = max(0, -steps), min(count, count - steps)
    return lax.ppermute(value, SPACE, [(i, i + steps) for i in range(first, last)])


def emit_faces(tiles, table_ref, face_refs):
    for index, ref in enumerate(face_refs):
        for b in range(BR):
            if index < 2:
                block = tiles[b, :, :, :].reshape(8, 8, 8, CH)[:, 7 * index]
            else:
                block = tiles[b, 56 * (index - 2) : 56 * (index - 2) + 8]
            ref[64 * b : 64 * b + 64] = block.reshape(64, CH).astype(BF16)
        ref[256:272] = table_ref[...]


def prep_kernel(field_ref, table_ref, tiles_ref, ym_ref, yp_ref, xm_ref, xp_ref):
    for b in range(BR):
        for k in range(4):
            start = VOX * b + 128 * k
            turned = field_ref[:, start : start + 128].astype(F32).T
            tiles_ref[b, 16 * k : 16 * k + 16] = turned.reshape(16, 8, CH)
    emit_faces(tiles_ref, table_ref, (ym_ref, yp_ref, xm_ref, xp_ref))


def prep(field, table):
    face = jax.ShapeDtypeStruct((272, CH), BF16)
    return pl.pallas_call(
        prep_kernel,
        out_shape=[jax.ShapeDtypeStruct((BR, 64, 8, CH), F32)] + [face] * 4,
        in_specs=[VMEM] * 2,
        out_specs=[VMEM] * 5,
        compiler_params=PARAMS,
    )(field, table)


def exchange(faces):
    ym, yp, xm, xp = faces
    from_low = shifted(yp, 1)
    from_high = shifted(ym, -1)

    def column(plane, p):
        rows = [plane[64 * b + 8 * p : 64 * b + 8 * p + 8] for b in range(BR)]
        return rows + [plane[256:272]]

    up = jnp.concatenate([xp] + column(from_low, 7) + column(from_high, 7), axis=0)
    down = jnp.concatenate([xm] + column(from_low, 0) + column(from_high, 0), axis=0)
    return from_low, from_high, shifted(up, ROWS), shifted(down, -ROWS)


def pool_index(neighbours, halo):
    low, high, left, right = halo
    tables = {
        (-1, -1): left[304:320],
        (-1, 0): left[256:272],
        (-1, 1): left[352:368],
        (0, -1): low[256:272],
        (0, 1): high[256:272],
        (1, -1): right[304:320],
        (1, 0): right[256:272],
        (1, 1): right[352:368],
    }
    rows = []
    for d, facing in enumerate(compass):
        rows.append(tables[facing][7 - d, :SLOTS].astype(jnp.int32) + BASE[facing])
    values = jnp.concatenate(rows)
    entry = neighbours - 1
    hit = entry[:, :, None] == jnp.arange(8 * SLOTS, dtype=jnp.int32)
    remote = jnp.sum(jnp.where(hit, values, 0), axis=2)
    found = jnp.where(entry >= 8 * SLOTS, entry - 8 * SLOTS, remote)
    return jnp.where(neighbours == 0, ZERO, found)


def fill_pool(pool, tiles_ref, halo_refs):
    low_ref, high_ref, left_ref, right_ref = halo_refs

    def plane(ref, start):
        return ref[start : start + 64].astype(F32).reshape(8, 8, CH)

    for b in range(BR):
        pool[b] = tiles_ref[b]
        pool[ZERO, 16 * b : 16 * b + 16] = jnp.zeros((16, 8, CH), F32)
        low = plane(low_ref, 64 * b)
        high = plane(high_ref, 64 * b)
        for p in range(8):
            pool[BASE[0, -1] + b, 8 * p + 7] = low[p]
            pool[BASE[0, 1] + b, 8 * p] = high[p]
        pool[BASE[-1, 0] + b, 56:64] = plane(left_ref, 64 * b)
        pool[BASE[1, 0] + b, 0:8] = plane(right_ref, 64 * b)
    for ref, ex, p in ((left_ref, -1, 7), (right_ref, 1, 0)):
        for ey, q, start in ((-1, 7, 272), (1, 0, 320)):
            rows = ref[start : start + 32].astype(F32).reshape(BR, 8, CH)
            for b in range(BR):
                pool[BASE[ex, ey] + b, 8 * p + q] = rows[b]


def build_windows(index_ref, pool, windows):
    row = lax.broadcasted_iota(jnp.int32, (8, CH), 0)
    first, last = row == 0, row == 7

    def place(entries, p, q, at_p, at_q):
        shifted_rows = ([], [], [])
        for b in range(BR):
            below = pool[entries[b][0], 8 * p + q]
            centre = pool[entries[b][1], 8 * p + q]
            above = pool[entries[b][2], 8 * p + q]
            shifted_rows[0].append(pltpu.roll(jnp.where(last, below, centre), 1, 0))
            shifted_rows[1].append(centre)
            shifted_rows[2].append(pltpu.roll(jnp.where(first, above, centre), 7, 0))
        for k in range(3):
            windows[k, at_p, at_q] = jnp.concatenate(shifted_rows[k], axis=0).astype(BF16)

    for ox in (-1, 0, 1):
        for oy in (-1, 0, 1):
            column = 9 * (ox + 1) + 3 * (oy + 1)
            entries = [[index_ref[b, column + k] for k in range(3)] for b in range(BR)]
            p_edge = 7 if ox < 0 else 0
            q_edge = 7 if oy < 0 else 0
            p_at = 0 if ox < 0 else 9
            q_at = 0 if oy < 0 else 9
            if ox == 0 and oy == 0:

                def plane_body(p, carry, entries=entries):
                    for q in range(8):
                        place(entries, p, q, p + 1, q + 1)
                    return carry

                lax.fori_loop(0, 8, plane_body, 0)
            elif ox == 0:

                def p_body(p, carry, entries=entries, q_edge=q_edge, q_at=q_at):
                    place(entries, p, q_edge, p + 1, q_at)
                    return carry

                lax.fori_loop(0, 8, p_body, 0)
            elif oy == 0:

                def q_body(q, carry, entries=entries, p_edge=p_edge, p_at=p_at):
                    place(entries, p_edge, q, p_at, q + 1)
                    return carry

                lax.fori_loop(0, 8, q_body, 0)
            else:
                place(entries, p_edge, q_edge, p_at, q_at)


def window(windows, k, at_p, j):
    return windows[k, at_p, j : j + 8].reshape(256, CH)


def forward_kernel(
    index_ref,
    chan_ref,
    tiles_ref,
    low_ref,
    high_ref,
    left_ref,
    right_ref,
    weight_ref,
    cotangent_ref,
    table_ref,
    output_ref,
    gradh_ref,
    ym_ref,
    yp_ref,
    xm_ref,
    xp_ref,
    kernel_grad_ref,
    pool,
    windows,
    cot_tiles,
    out_tiles,
    out_turned,
    grad_rows,
    narrow,
    sums,
):
    fill_pool(pool, tiles_ref, (low_ref, high_ref, left_ref, right_ref))
    build_windows(index_ref, pool, windows)
    for b in range(BR):
        for k in range(4):
            start = VOX * b + 128 * k
            turned = cotangent_ref[:, start : start + 128].astype(F32).T
            cot_tiles[b, 16 * k : 16 * k + 16] = turned.reshape(16, 8, CH)

    def tap_weight(tap):
        return jnp.concatenate([weight_ref[s, tap] for s in range(4)], axis=0)

    def conv_body(p, carry):
        total = None
        for first in range(0, TAPS, 2):
            taps = range(first, min(first + 2, TAPS))
            left = [window(windows, t % 3, p + t // 9, t // 3 % 3) for t in taps]
            right = [tap_weight(t) for t in taps]
            term = jnp.dot(
                jnp.concatenate(left, axis=1), jnp.concatenate(right, axis=0), preferred_element_type=F32
            )
            total = term if total is None else total + term
        hidden = total.reshape(8, BR, 8, CH)
        for b in range(BR):
            h = hidden[:, b]
            feat = tiles_ref[b, pl.ds(8 * p, 8)]
            cot = cot_tiles[b, pl.ds(8 * p, 8)]
            sig = jax.nn.sigmoid(h)
            out_tiles[b, pl.ds(8 * p, 8)] = feat + h * sig
            grad = (cot * sig * (1.0 + h * (1.0 - sig))).astype(BF16).astype(F32)
            gradh_ref[b, pl.ds(8 * p, 8)] = grad
        return carry

    lax.fori_loop(0, 8, conv_body, 0)

    for b in range(BR):
        for k in range(4):
            start = VOX * b + 128 * k
            block = out_tiles[b, 16 * k : 16 * k + 16].reshape(128, CH)
            out_turned[:, start : start + 128] = block.T
    own = pl.multiple_of(chan_ref[0] * 32, 32)
    output_ref[...] = out_turned[pl.ds(own, 32), :].astype(BF16)
    emit_faces(gradh_ref, table_ref, (ym_ref, yp_ref, xm_ref, xp_ref))

    lane = lax.broadcasted_iota(jnp.int32, (CH, CH), 1)
    channel = lax.broadcasted_iota(jnp.int32, (CH, CH), 0)
    pick = [
        jnp.where((lane - 32 * k == channel - own) & (lane >= 32 * k) & (lane < 32 * k + 32), 1.0, 0.0).astype(BF16)
        for k in range(3)
    ]
    picks = jnp.concatenate(pick, axis=0)

    def narrow_body(p, carry):
        rows = [windows[k, p].reshape(320, CH) for k in range(3)]
        small = jnp.dot(jnp.concatenate(rows, axis=1), picks, preferred_element_type=F32)
        narrow[p] = small.astype(BF16).reshape(10, 32, CH)
        return carry

    lax.fori_loop(0, 10, narrow_body, 0)

    def turn_body(p, carry):
        parts = [gradh_ref[b, pl.ds(8 * p, 8)] for b in range(BR)]
        rows = jnp.stack(parts, axis=1).reshape(256, CH)
        for k in range(2):
            grad_rows[p, :, 128 * k : 128 * k + 128] = rows[128 * k : 128 * k + 128].T.astype(BF16)
        return carry

    lax.fori_loop(0, 8, turn_body, 0)

    sums[...] = jnp.zeros_like(sums)

    def sum_body(p, carry):
        left = grad_rows[p]
        for pair in range(9):
            i, j = pair // 3, pair % 3
            right = narrow[p + i, j : j + 8].reshape(256, CH)
            sums[pair] += jnp.dot(left, right, preferred_element_type=F32)
        return carry

    lax.fori_loop(0, 8, sum_body, 0)
    for pair in range(9):
        kernel_grad_ref[96 * pair : 96 * pair + 96] = sums[pair].T[:96]
    kernel_grad_ref[864:896] = jnp.zeros((32, CH), F32)


def forward(index, chan, tiles, halo, weight, cotangent, table):
    face = jax.ShapeDtypeStruct((272, CH), BF16)
    return pl.pallas_call(
        forward_kernel,
        out_shape=[
            jax.ShapeDtypeStruct((32, BR * VOX), BF16),
            jax.ShapeDtypeStruct((BR, 64, 8, CH), F32),
            face,
            face,
            face,
            face,
            jax.ShapeDtypeStruct((896, CH), F32),
        ],
        in_specs=[SMEM] * 2 + [VMEM] * 8,
        out_specs=[VMEM] * 7,
        scratch_shapes=[
            pltpu.VMEM((37, 64, 8, CH), F32),
            pltpu.VMEM((3, 10, 10, 32, CH), BF16),
            pltpu.VMEM((BR, 64, 8, CH), F32),
            pltpu.VMEM((BR, 64, 8, CH), F32),
            pltpu.VMEM((CH, BR * VOX), F32),
            pltpu.VMEM((8, CH, 256), BF16),
            pltpu.VMEM((10, 10, 32, CH), BF16),
            pltpu.VMEM((9, CH, CH), F32),
        ],
        compiler_params=PARAMS,
    )(index, chan, tiles, *halo, weight, cotangent, table)


def backward_kernel(
    index_ref,
    tiles_ref,
    low_ref,
    high_ref,
    left_ref,
    right_ref,
    weight_ref,
    cotangent_ref,
    grad_ref,
    pool,
    windows,
    result,
):
    fill_pool(pool, tiles_ref, (low_ref, high_ref, left_ref, right_ref))
    build_windows(index_ref, pool, windows)

    def conv_body(p, carry):
        total = None
        for first in range(0, TAPS, 2):
            taps = range(first, min(first + 2, TAPS))
            left = [window(windows, 2 - t % 3, p + 2 - t // 9, 2 - t // 3 % 3) for t in taps]
            right = [weight_ref[t] for t in taps]
            term = lax.dot_general(
                jnp.concatenate(left, axis=1),
                jnp.concatenate(right, axis=1),
                (((1,), (1,)), ((), ())),
                preferred_element_type=F32,
            )
            total = term if total is None else total + term
        rows = total.reshape(8, BR, 8, 32)
        for b in range(BR):
            result[b, pl.ds(8 * p, 8)] = rows[:, b]
        return carry

    lax.fori_loop(0, 8, conv_body, 0)
    for b in range(BR):
        for k in range(4):
            start = VOX * b + 128 * k
            block = result[b, 16 * k : 16 * k + 16].reshape(128, 32)
            summed = cotangent_ref[:, start : start + 128].astype(F32) + block.T
            grad_ref[:, start : start + 128] = summed.astype(BF16)


def backward(index, tiles, halo, weight, cotangent):
    return pl.pallas_call(
        backward_kernel,
        out_shape=jax.ShapeDtypeStruct((32, BR * VOX), BF16),
        in_specs=[SMEM] + [VMEM] * 7,
        out_specs=VMEM,
        scratch_shapes=[
            pltpu.VMEM((37, 64, 8, CH), F32),
            pltpu.VMEM((3, 10, 10, 32, CH), BF16),
            pltpu.VMEM((BR, 64, 8, 32), F32),
        ],
        compiler_params=PARAMS,
    )(index, tiles, *halo, weight, cotangent)


def ring_gather(value, axis):
    count = lax.axis_size(axis)
    blocks = [value]
    for step in range(1, count):
        blocks.append(lax.ppermute(value, axis, [(i, (i + step) % count) for i in range(count)]))
    return blocks


def spread(value, axis):
    count = lax.axis_size(axis)
    copies = jnp.broadcast_to(value[None], (count,) + value.shape)
    return lax.all_to_all(copies, axis, split_axis=0, concat_axis=0, tiled=True)


def reduce_space(partial):
    pieces = lax.all_to_all(partial.reshape(8, 112, CH), XC, split_axis=0, concat_axis=0, tiled=True)
    mine = jnp.sum(pieces, axis=0)
    column = jnp.sum(spread(mine, "z"), axis=0)
    return spread(column, XC).reshape(896, CH)[:864]


def per_device(features, weight, cotangent, neighbours, send_slots):
    feat_own = features.reshape(32, BR * VOX)
    cot_own = cotangent.reshape(32, BR * VOX)
    table = jnp.pad(send_slots.astype(BF16), ((0, 8), (0, CH - SLOTS)))
    feat_all = lax.all_gather(feat_own, "chan", axis=0, tiled=True)
    weight_all = lax.all_gather(weight, "chan", axis=0, tiled=False)
    cot_all = lax.all_gather(cot_own, "chan", axis=0, tiled=True)
    chan = lax.axis_index("chan").astype(jnp.int32).reshape(1)
    tiles, *faces = prep(feat_all, table)
    halo = exchange(faces)
    index = pool_index(neighbours, halo)
    out, grad_tiles, *rest = forward(index, chan, tiles, halo, weight_all, cot_all, table)
    grad_faces, partial = rest[:4], rest[4]
    grad_halo = exchange(grad_faces)
    grad_weight = reduce_space(partial)
    grad_input = backward(index, grad_tiles, grad_halo, weight, cot_own)
    return (
        out.reshape(32, BR, VOX),
        grad_input.reshape(32, BR, VOX),
        grad_weight.reshape(TAPS, 32, CH),
    )


def solution(mesh):
    fine = Mesh(mesh.devices.reshape(4, 8, 2, 4), ("x", "z", "core", "chan"))
    return jax.shard_map(
        per_device,
        mesh=fine,
        in_specs=(
            P("chan", SPACE, None),
            P(None, "chan", None),
            P("chan", SPACE, None),
            P(SPACE, None),
            P(SPACE, None),
        ),
        out_specs=(P("chan", SPACE, None), P("chan", SPACE, None), P(None, "chan", None)),
        check_vma=False,
    )
```

```python
import jax
import jax.numpy as jnp
from jax import lax
from jax.experimental import pallas as pl
from jax.experimental.pallas import tpu as pltpu
from jax.sharding import Mesh, PartitionSpec as P

ROWS = 4
CH = 128
OWN = 32
BR = 4
VOX = 512
TAPS = 27
SLOTS = 8
F32 = jnp.float32
BF16 = jnp.bfloat16
SPACE = ("x", "z", "core")
VMEM = pl.BlockSpec(memory_space=pltpu.VMEM)
SMEM = pl.BlockSpec(memory_space=pltpu.SMEM)
LIMIT = 56 * 2**20

compass = ((-1, -1), (-1, 0), (-1, 1), (0, -1), (0, 1), (1, -1), (1, 0), (1, 1))
SIDE_M, SIDE_N, SIDE_L, SIDE_R, SIDE_LM, SIDE_LN, SIDE_RM, SIDE_RN, ZERO = range(4, 40, 4)


def params():
    return pltpu.CompilerParams(vmem_limit_bytes=LIMIT)


def cost(flops, moved):
    return pl.CostEstimate(flops=flops, bytes_accessed=moved, transcendentals=0)


def shifted(value, steps):
    count = lax.axis_size(SPACE)
    first, last = max(0, -steps), min(count, count - steps)
    return lax.ppermute(value, SPACE, [(i, i + steps) for i in range(first, last)])


def emit_faces(core, tiles, table_ref, face_refs):
    for index, ref in enumerate(face_refs):
        for b in range(BR):
            if index == 0:
                rows = [tiles[b, 8 * p + 7 * (1 - core)] for p in range(8)]
            elif index == 1:
                rows = [tiles[b, 8 * p + 7 * core] for p in range(8)]
            else:
                rows = [tiles[b, 56 * (index - 2) + q] for q in range(8)]
            ref[64 * b : 64 * b + 64] = jnp.concatenate(rows, axis=0).astype(BF16)
        ref[256:272] = jnp.zeros((16, CH), BF16) if table_ref is None else table_ref[...]


def prep_kernel(core_ref, own_ref, ring1_ref, ring2_ref, ring3_ref, table_ref, tiles_ref, *face_refs):
    for b in range(BR):
        for k in range(4):
            start = VOX * b + 128 * k
            parts = [ref[:, start : start + 128] for ref in (own_ref, ring1_ref, ring2_ref, ring3_ref)]
            turned = jnp.concatenate(parts, axis=0).astype(F32).T
            tiles_ref[b, 16 * k : 16 * k + 16] = turned.reshape(16, 8, CH)
    emit_faces(core_ref[0], tiles_ref, table_ref, face_refs)


def prep(core, blocks, table):
    face = jax.ShapeDtypeStruct((272, CH), BF16)
    return pl.pallas_call(
        prep_kernel,
        out_shape=[jax.ShapeDtypeStruct((BR, 64, 8, CH), F32)] + [face] * 4,
        in_specs=[SMEM] + [VMEM] * 5,
        out_specs=[VMEM] * 5,
        compiler_params=params(),
        cost_estimate=cost(0, 2**22),
    )(core, *blocks, table)


def turn_kernel(chan_ref, own_ref, ring1_ref, ring2_ref, ring3_ref, tiles_ref, whole):
    for step, ref in enumerate((own_ref, ring1_ref, ring2_ref, ring3_ref)):
        block = lax.rem(chan_ref[0] + 4 - step, 4)
        whole[pl.ds(pl.multiple_of(block * OWN, OWN), OWN), :] = ref[...].astype(F32)
    for b in range(BR):
        for k in range(4):
            start = VOX * b + 128 * k
            tiles_ref[b, 16 * k : 16 * k + 16] = whole[:, start : start + 128].T.reshape(16, 8, CH)


def turn(chan, blocks):
    return pl.pallas_call(
        turn_kernel,
        out_shape=jax.ShapeDtypeStruct((BR, 64, 8, CH), F32),
        in_specs=[SMEM] + [VMEM] * 4,
        out_specs=VMEM,
        scratch_shapes=[pltpu.VMEM((CH, BR * VOX), F32)],
        compiler_params=params(),
        cost_estimate=cost(0, 2**22),
    )(chan, *blocks)


def column(plane, p):
    rows = [plane[64 * b + 8 * p : 64 * b + 8 * p + 8] for b in range(BR)]
    return rows + [plane[256:272]]


def exchange(faces):
    face_m, face_n, low, high = faces
    count = lax.axis_size(SPACE)
    across = [(s, s + 1) for s in range(count) if s % 4 == 1] + [(s, s - 1) for s in range(count) if s % 4 == 2]
    side_n = lax.ppermute(face_n, SPACE, across)
    side_m = lax.ppermute(face_m, "core", [(0, 1), (1, 0)])
    up = jnp.concatenate([high] + column(side_m, 7) + column(side_n, 7), axis=0)
    down = jnp.concatenate([low] + column(side_m, 0) + column(side_n, 0), axis=0)
    return side_m, side_n, shifted(up, ROWS), shifted(down, -ROWS)


def pool_index(neighbours, core, halo):
    side_m, side_n, left, right = halo
    tables = {
        SIDE_M: side_m[256:272],
        SIDE_N: side_n[256:272],
        SIDE_L: left[256:272],
        SIDE_R: right[256:272],
        SIDE_LM: left[304:320],
        SIDE_LN: left[352:368],
        SIDE_RM: right[304:320],
        SIDE_RN: right[352:368],
    }
    ends = {-1: (SIDE_LM, SIDE_LN), 0: (SIDE_M, SIDE_N), 1: (SIDE_RM, SIDE_RN)}

    def row(side, d):
        return tables[side][7 - d, :SLOTS].astype(jnp.int32) + side

    rows = []
    for d, (ex, ey) in enumerate(compass):
        if ey == 0:
            rows.append(row(SIDE_L if ex < 0 else SIDE_R, d))
        else:
            near, far = ends[ex] if ey > 0 else ends[ex][::-1]
            rows.append(jnp.where(core == 0, row(near, d), row(far, d)))
    values = jnp.concatenate(rows)
    entry = neighbours - 1
    hit = entry[:, :, None] == jnp.arange(8 * SLOTS, dtype=jnp.int32)
    remote = jnp.sum(jnp.where(hit, values, 0), axis=2)
    found = jnp.where(entry >= 8 * SLOTS, entry - 8 * SLOTS, remote)
    return jnp.where(neighbours == 0, ZERO, found)


def fill_pool(core, pool, tiles_ref, halo_refs):
    side_m, side_n, left, right = halo_refs
    q_m, q_n = 7 * core, 7 * (1 - core)

    def plane(ref, start):
        return ref[start : start + 64].astype(F32).reshape(8, 8, CH)

    for b in range(BR):
        for first in range(0, 64, 8):
            pool[b, first : first + 8] = tiles_ref[b, first : first + 8]
            pool[ZERO, first : first + 8] = jnp.zeros((8, 8, CH), F32)
        for ref, side, q in ((side_m, SIDE_M, q_m), (side_n, SIDE_N, q_n)):
            rows = plane(ref, 64 * b)
            for p in range(8):
                pool[side + b, 8 * p + q] = rows[p]
        pool[SIDE_L + b, 56:64] = plane(left, 64 * b)
        pool[SIDE_R + b, 0:8] = plane(right, 64 * b)
    for ref, sides, p in ((left, (SIDE_LM, SIDE_LN), 7), (right, (SIDE_RM, SIDE_RN), 0)):
        for side, q, start in ((sides[0], q_m, 272), (sides[1], q_n, 320)):
            rows = ref[start : start + 32].astype(F32).reshape(BR, 8, CH)
            for b in range(BR):
                pool[side + b, 8 * p + q] = rows[b]


def three_shifts(entries, pool, p, q):
    row = lax.broadcasted_iota(jnp.int32, (8, CH), 0)
    first, last = row == 0, row == 7
    shifts = ([], [], [])
    for b in range(BR):
        below = pool[entries[b][0], 8 * p + q]
        centre = pool[entries[b][1], 8 * p + q]
        above = pool[entries[b][2], 8 * p + q]
        shifts[0].append(pltpu.roll(jnp.where(last, below, centre), 1, 0))
        shifts[1].append(centre)
        shifts[2].append(pltpu.roll(jnp.where(first, above, centre), 7, 0))
    return [jnp.concatenate(rows, axis=0).astype(BF16) for rows in shifts]


def inner_windows(neighbours_ref, tiles_ref, zero, windows):
    zero[...] = jnp.zeros_like(zero)
    blank = jnp.zeros((10, 32, CH), BF16)
    for k in range(3):
        windows[k, 0] = blank
        windows[k, 9] = blank
        for p in range(1, 9):
            windows[k, p, 0] = blank[0]
            windows[k, p, 9] = blank[0]
    for b in range(BR):
        zero[b] = tiles_ref[b]
    entries = []
    for b in range(BR):
        found = [neighbours_ref[b, 12 + k] for k in range(3)]
        entries.append([jnp.where(e > 64, e - 65, 4) for e in found])

    def body(p, carry):
        for q in range(8):
            for k, rows in enumerate(three_shifts(entries, zero, p, q)):
                windows[k, p + 1, q + 1] = rows
        return carry

    lax.fori_loop(0, 8, body, 0)


def margin_windows(index_ref, pool, ends, strips):
    blank = jnp.zeros((32, CH), BF16)
    for ox in (-1, 0, 1):
        for oy in (-1, 0, 1):
            if ox == 0 and oy == 0:
                continue
            start = 9 * (ox + 1) + 3 * (oy + 1)
            entries = [[index_ref[b, start + k] for k in range(3)] for b in range(BR)]
            for i in range(8):
                p = i if ox == 0 else (7 if ox < 0 else 0)
                q = i if oy == 0 else (7 if oy < 0 else 0)
                for k, rows in enumerate(three_shifts(entries, pool, p, q)):
                    if ox == 0:
                        strips[(oy + 1) // 2, k, p + 1] = rows
                    else:
                        ends[(ox + 1) // 2, k, q + 1 if oy == 0 else (0 if oy < 0 else 9)] = rows
                if ox != 0 and oy != 0:
                    break
    for side in range(2):
        for k in range(3):
            strips[side, k, 0] = blank
            strips[side, k, 9] = blank


def conv_sum(pairs):
    total = None
    for first in range(0, len(pairs), 2):
        group = pairs[first : first + 2]
        left = jnp.concatenate([rows for rows, _ in group], axis=1)
        right = jnp.concatenate([tap for _, tap in group], axis=0)
        term = jnp.dot(left, right, preferred_element_type=F32)
        total = term if total is None else total + term
    return total


def turned_sum(pairs):
    total = None
    for first in range(0, len(pairs), 2):
        group = pairs[first : first + 2]
        left = jnp.concatenate([rows for rows, _ in group], axis=1)
        right = jnp.concatenate([tap for _, tap in group], axis=1)
        term = lax.dot_general(left, right, (((1,), (1,)), ((), ())), preferred_element_type=F32)
        total = term if total is None else total + term
    return total


def inner_sum(windows, summed, tap_weight, sign, p):
    pairs = []
    for t in range(TAPS):
        ox, oy, oz = (sign * (v - 1) for v in (t // 9, t // 3 % 3, t % 3))
        rows = windows[oz + 1, p + ox + 1, oy + 1 : oy + 9].reshape(256, CH)
        pairs.append((rows, tap_weight(t)))
    return summed(pairs)


def margin_sums(ends, strips, summed, tap_weight, sign):
    added = []
    for side in range(2):
        along_x, along_y = [], []
        for t in range(TAPS):
            ox, oy, oz = (sign * (v - 1) for v in (t // 9, t // 3 % 3, t % 3))
            if ox == 2 * side - 1:
                along_x.append((ends[side, oz + 1, oy + 1 : oy + 9].reshape(256, CH), tap_weight(t)))
            if oy == 2 * side - 1:
                along_y.append((strips[side, oz + 1, ox + 1 : ox + 9].reshape(256, CH), tap_weight(t)))
        added.append((summed(along_x), summed(along_y)))
    return added


def picks():
    lane = lax.broadcasted_iota(jnp.int32, (CH, CH), 1)
    channel = lax.broadcasted_iota(jnp.int32, (CH, CH), 0)
    parts = [
        jnp.where((lane - OWN * k == channel) & (channel < OWN), 1.0, 0.0).astype(BF16) for k in range(3)
    ]
    return jnp.concatenate(parts, axis=0)


def narrowed(rows):
    return jnp.dot(jnp.concatenate(rows, axis=1), picks(), preferred_element_type=F32).astype(BF16)


def inner_kernel(nb_ref, tiles_ref, w0_ref, w1_ref, w2_ref, w3_ref, hidden_ref, narrow_ref, zero, windows):
    inner_windows(nb_ref, tiles_ref, zero, windows)
    weights = (w0_ref, w1_ref, w2_ref, w3_ref)

    def tap_weight(t):
        return jnp.concatenate([ref[t] for ref in weights], axis=0)

    def body(p, carry):
        hidden_ref[p] = inner_sum(windows, conv_sum, tap_weight, 1, p).reshape(8, 32, CH)
        rows = [windows[k, p + 1, 1:9].reshape(256, CH) for k in range(3)]
        narrow_ref[p] = narrowed(rows).reshape(8, 32, CH)
        return carry

    lax.fori_loop(0, 8, body, 0)


def inner(neighbours, tiles, weights):
    return pl.pallas_call(
        inner_kernel,
        out_shape=[jax.ShapeDtypeStruct((8, 8, 32, CH), F32), jax.ShapeDtypeStruct((8, 8, 32, CH), BF16)],
        in_specs=[SMEM] + [VMEM] * 5,
        out_specs=[VMEM] * 2,
        scratch_shapes=[
            pltpu.VMEM((5, 64, 8, CH), F32),
            pltpu.VMEM((3, 10, 10, 32, CH), BF16),
        ],
        compiler_params=params(),
        cost_estimate=cost(2 * 27 * CH * CH * 2048, 2**24),
    )(neighbours, tiles, *weights)


def gate_kernel(
    index_ref,
    place_ref,
    tiles_ref,
    cot_ref,
    inner_ref,
    inner_narrow_ref,
    side_m_ref,
    side_n_ref,
    left_ref,
    right_ref,
    w0_ref,
    w1_ref,
    w2_ref,
    w3_ref,
    gated_ref,
    grad_ref,
    face_m_ref,
    face_n_ref,
    low_ref,
    high_ref,
    keep_ref,
    send_ref,
    pool,
    ends,
    strips,
    hidden,
    narrow,
    grad_rows,
    sums,
):
    core = place_ref[0]
    weights = (w0_ref, w1_ref, w2_ref, w3_ref)
    fill_pool(core, pool, tiles_ref, (side_m_ref, side_n_ref, left_ref, right_ref))
    margin_windows(index_ref, pool, ends, strips)

    def tap_weight(t):
        return jnp.concatenate([ref[t] for ref in weights], axis=0)

    for p in range(8):
        hidden[p] = inner_ref[p]
        narrow[p + 1, 1:9] = inner_narrow_ref[p]
    for side, (along_x, along_y) in enumerate(margin_sums(ends, strips, conv_sum, tap_weight, 1)):
        hidden[7 * side] += along_x.reshape(8, 32, CH)
        for p in range(8):
            hidden[p, 7 * side] += along_y[32 * p : 32 * p + 32]
        rows = [ends[side, k].reshape(320, CH) for k in range(3)]
        narrow[9 * side] = narrowed(rows).reshape(10, 32, CH)
        rows = [strips[side, k, 1:9].reshape(256, CH) for k in range(3)]
        small = narrowed(rows)
        for p in range(8):
            narrow[p + 1, 9 * side] = small[32 * p : 32 * p + 32]

    def gate_body(p, carry):
        h = hidden[p].reshape(8, BR, 8, CH)
        grads = []
        for b in range(BR):
            part = h[:, b]
            cot = cot_ref[b, pl.ds(8 * p, 8)]
            sig = jax.nn.sigmoid(part)
            gated_ref[b, pl.ds(8 * p, 8)] = part * sig
            grad = (cot * sig * (1.0 + part * (1.0 - sig))).astype(BF16).astype(F32)
            grad_ref[b, pl.ds(8 * p, 8)] = grad
            grads.append(grad)
        rows = jnp.stack(grads, axis=1).reshape(256, CH)
        for k in range(2):
            grad_rows[p, :, 128 * k : 128 * k + 128] = rows[128 * k : 128 * k + 128].T.astype(BF16)
        return carry

    lax.fori_loop(0, 8, gate_body, 0)
    emit_faces(core, grad_ref, None, (face_m_ref, face_n_ref, low_ref, high_ref))

    for i in range(3):

        def sum_body(p, carry, i=i):
            left = grad_rows[p]
            right = [narrow[p + i, j : j + 8].reshape(256, CH) for j in range(3)]
            return carry + jnp.dot(left, jnp.concatenate(right, axis=1), preferred_element_type=F32)

        total = lax.fori_loop(0, 8, sum_body, jnp.zeros((CH, 3 * CH), F32))
        for j in range(3):
            start = 96 * (3 * i + j)
            sums[start : start + 96] = total[:, CH * j : CH * j + CH].T[:96]
    sums[864:896] = jnp.zeros((32, CH), F32)
    keep_ref[...] = sums[pl.ds(pl.multiple_of(448 * core, 8), 448), :]
    send_ref[...] = sums[pl.ds(pl.multiple_of(448 * (1 - core), 8), 448), :]


def gate(index, core, tiles, cot, hidden, narrow, halo, weights):
    face = jax.ShapeDtypeStruct((272, CH), BF16)
    half = jax.ShapeDtypeStruct((448, CH), F32)
    field = jax.ShapeDtypeStruct((BR, 64, 8, CH), F32)
    return pl.pallas_call(
        gate_kernel,
        out_shape=[field, field, face, face, face, face, half, half],
        in_specs=[SMEM] * 2 + [VMEM] * 12,
        out_specs=[VMEM] * 8,
        scratch_shapes=[
            pltpu.VMEM((40, 64, 8, CH), F32),
            pltpu.VMEM((2, 3, 10, 32, CH), BF16),
            pltpu.VMEM((2, 3, 10, 32, CH), BF16),
            pltpu.VMEM((8, 8, 32, CH), F32),
            pltpu.VMEM((10, 10, 32, CH), BF16),
            pltpu.VMEM((8, CH, 256), BF16),
            pltpu.VMEM((896, CH), F32),
        ],
        compiler_params=params(),
        cost_estimate=cost(2 * 27 * CH * CH * 1024, 2**24),
    )(index, core, tiles, cot, hidden, narrow, *halo, *weights)


def back_inner_kernel(nb_ref, chan_ref, tiles_ref, weight_ref, gated_ref, feat_ref, part_ref, out_ref, zero, windows, turned):
    inner_windows(nb_ref, tiles_ref, zero, windows)

    def body(p, carry):
        part_ref[p] = inner_sum(windows, turned_sum, lambda t: weight_ref[t], -1, p).reshape(8, 32, OWN)
        return carry

    lax.fori_loop(0, 8, body, 0)
    own = pl.multiple_of(chan_ref[0] * OWN, OWN)
    for b in range(BR):
        for k in range(4):
            start = VOX * b + 128 * k
            turned[:, start : start + 128] = gated_ref[b, 16 * k : 16 * k + 16].reshape(128, CH).T
    out_ref[...] = (feat_ref[...].astype(F32) + turned[pl.ds(own, OWN), :]).astype(BF16)


def back_inner(neighbours, chan, tiles, weight, gated, features):
    return pl.pallas_call(
        back_inner_kernel,
        out_shape=[
            jax.ShapeDtypeStruct((8, 8, 32, OWN), F32),
            jax.ShapeDtypeStruct((OWN, BR * VOX), BF16),
        ],
        in_specs=[SMEM] * 2 + [VMEM] * 4,
        out_specs=[VMEM] * 2,
        scratch_shapes=[
            pltpu.VMEM((5, 64, 8, CH), F32),
            pltpu.VMEM((3, 10, 10, 32, CH), BF16),
            pltpu.VMEM((CH, BR * VOX), F32),
        ],
        compiler_params=params(),
        cost_estimate=cost(2 * 27 * CH * CH * 2048, 2**24),
    )(neighbours, chan, tiles, weight, gated, features)


def back_margin_kernel(
    index_ref,
    place_ref,
    tiles_ref,
    side_m_ref,
    side_n_ref,
    left_ref,
    right_ref,
    weight_ref,
    part_ref,
    cot_ref,
    grad_ref,
    pool,
    ends,
    strips,
    result,
):
    fill_pool(place_ref[0], pool, tiles_ref, (side_m_ref, side_n_ref, left_ref, right_ref))
    margin_windows(index_ref, pool, ends, strips)
    for p in range(8):
        result[p] = part_ref[p]
    for side, (along_x, along_y) in enumerate(margin_sums(ends, strips, turned_sum, lambda t: weight_ref[t], -1)):
        result[7 * side] += along_x.reshape(8, 32, OWN)
        for p in range(8):
            result[p, 7 * side] += along_y[32 * p : 32 * p + 32]
    for b in range(BR):
        for k in range(4):
            start = VOX * b + 128 * k
            block = result[2 * k : 2 * k + 2, :, 8 * b : 8 * b + 8, :].reshape(128, OWN)
            summed = cot_ref[:, start : start + 128].astype(F32) + block.T
            grad_ref[:, start : start + 128] = summed.astype(BF16)


def back_margin(index, core, tiles, halo, weight, part, cotangent):
    return pl.pallas_call(
        back_margin_kernel,
        out_shape=jax.ShapeDtypeStruct((OWN, BR * VOX), BF16),
        in_specs=[SMEM] * 2 + [VMEM] * 8,
        out_specs=VMEM,
        scratch_shapes=[
            pltpu.VMEM((40, 64, 8, CH), F32),
            pltpu.VMEM((2, 3, 10, 32, CH), BF16),
            pltpu.VMEM((2, 3, 10, 32, CH), BF16),
            pltpu.VMEM((8, 8, 32, OWN), F32),
        ],
        compiler_params=params(),
        cost_estimate=cost(2 * 27 * CH * CH * 512, 2**23),
    )(index, core, tiles, *halo, weight, part, cotangent)


def ring_gather(value, axis):
    count = lax.axis_size(axis)
    blocks = [value]
    for step in range(1, count):
        blocks.append(lax.ppermute(value, axis, [(i, (i + step) % count) for i in range(count)]))
    return blocks


def swapped(value, axis, partner):
    return lax.ppermute(value, axis, list(enumerate(partner)))


X_NEAR, X_FAR = (1, 0, 3, 2), (3, 2, 1, 0)
Z_PAIRS = ((1, 0, 3, 2, 5, 4, 7, 6), (2, 3, 0, 1, 6, 7, 4, 5), (6, 7, 4, 5, 2, 3, 0, 1))


def halve(value, bit, partner):
    halves = value.reshape(2, value.shape[0] // 2, CH)
    keep = lax.dynamic_index_in_dim(halves, bit, 0, keepdims=False)
    send = lax.dynamic_index_in_dim(halves, 1 - bit, 0, keepdims=False)
    return keep + swapped(send, "x", partner)


def place_kernel(me_ref, one_ref, two_ref, four_ref, eight_ref, out_ref):
    for t in range(8):
        if t < 1:
            rows = one_ref[...]
        elif t < 2:
            rows = two_ref[...]
        elif t < 4:
            rows = four_ref[112 * (t - 2) : 112 * (t - 1)]
        else:
            rows = eight_ref[112 * (t - 4) : 112 * (t - 3)]
        at = me_ref[t]
        start = pl.multiple_of(112 * at, 8)

        @pl.when(at < 7)
        def _():
            out_ref[pl.ds(start, 112), :] = rows

        @pl.when(at == 7)
        def _():
            out_ref[pl.ds(start, 80), :] = rows[:80]


def after(value, *others):
    return lax.optimization_barrier((value,) + others)[0]


def reduce_space(keep, send, beside):
    x = lax.axis_index("x")
    core = lax.axis_index("core")
    high = x // 2
    low = (x ^ (x // 2)) & 1
    value = keep + swapped(send, "core", (1, 0))
    value = halve(value, high, X_FAR)
    value = halve(after(value, *beside[0]), low, X_NEAR)
    for step, partner in enumerate(Z_PAIRS):
        value = after(value, *beside[step + 1])
        value = value + swapped(value, "z", partner)
    value = after(value, *beside[4])
    two = swapped(value, "x", X_NEAR)
    pair = jnp.concatenate([value, two], axis=0)
    four = swapped(pair, "x", X_FAR)
    quad = jnp.concatenate([pair, four], axis=0)
    eight = swapped(quad, "core", (1, 0))
    me = 4 * core + 2 * high + low
    return pl.pallas_call(
        place_kernel,
        out_shape=jax.ShapeDtypeStruct((864, CH), F32),
        in_specs=[SMEM] + [VMEM] * 4,
        out_specs=VMEM,
        compiler_params=params(),
        cost_estimate=cost(0, 2**20),
    )(me ^ jnp.arange(8, dtype=jnp.int32), value, two, four, eight)


def per_device(features, weight, cotangent, neighbours, send_slots):
    core = lax.axis_index("core").astype(jnp.int32)
    chan = lax.axis_index("chan").astype(jnp.int32).reshape(1)
    core_at = core.reshape(1)
    feat_own = features.reshape(OWN, BR * VOX)
    cot_own = cotangent.reshape(OWN, BR * VOX)
    table = jnp.pad(send_slots.astype(BF16), ((0, 8), (0, CH - SLOTS)))
    feat_blocks = ring_gather(feat_own, "chan")
    weights = ring_gather(weight, "chan")

    tiles, *faces = prep(core_at, feat_blocks, table)
    halo = exchange(faces)
    cot_blocks = ring_gather(after(cot_own, *halo[:2]), "chan")
    hidden, narrow = inner(neighbours, tiles, weights)
    cot = turn(chan, cot_blocks)
    index = pool_index(neighbours, core, halo)
    gated, grads, face_m, face_n, low, high, keep, send = gate(index, core_at, tiles, cot, hidden, narrow, halo, weights)
    grad_halo = exchange((face_m, face_n, low, high))
    part, out = back_inner(neighbours, chan, grads, weight, gated, feat_own)
    grad_input = back_margin(index, core_at, grads, grad_halo, weight, part, cot_own)
    grad_weight = reduce_space(keep, send, (grad_halo[:2], (part,), grad_halo[2:], (grad_input,), ()))
    return (
        out.reshape(OWN, BR, VOX),
        grad_input.reshape(OWN, BR, VOX),
        grad_weight.reshape(TAPS, OWN, CH),
    )


def solution(mesh):
    fine = Mesh(mesh.devices.reshape(4, 8, 2, 4), ("x", "z", "core", "chan"))
    return jax.shard_map(
        per_device,
        mesh=fine,
        in_specs=(
            P("chan", SPACE, None),
            P(None, "chan", None),
            P("chan", SPACE, None),
            P(SPACE, None),
            P(SPACE, None),
        ),
        out_specs=(P("chan", SPACE, None), P("chan", SPACE, None), P(None, "chan", None)),
        check_vma=False,
    )
```

```python
import jax
import jax.numpy as jnp
from jax import lax
from jax.experimental import pallas as pl
from jax.experimental.pallas import tpu as pltpu
from jax.sharding import Mesh, PartitionSpec as P

ROWS = 4
CH = 128
OWN = 32
BR = 4
VOX = 512
TAPS = 27
SLOTS = 8
F32 = jnp.float32
BF16 = jnp.bfloat16
SPACE = ("x", "z", "core")
VMEM = pl.BlockSpec(memory_space=pltpu.VMEM)
SMEM = pl.BlockSpec(memory_space=pltpu.SMEM)

compass = ((-1, -1), (-1, 0), (-1, 1), (0, -1), (0, 1), (1, -1), (1, 0), (1, 1))
SIDE_M, SIDE_N, SIDE_L, SIDE_R, SIDE_LM, SIDE_LN, SIDE_RM, SIDE_RN, ZERO = range(4, 40, 4)


def params(mib):
    return pltpu.CompilerParams(vmem_limit_bytes=mib * 2**20)


def cost(flops, moved):
    return pl.CostEstimate(flops=flops, bytes_accessed=moved, transcendentals=0)


def shifted(value, steps):
    count = lax.axis_size(SPACE)
    first, last = max(0, -steps), min(count, count - steps)
    return lax.ppermute(value, SPACE, [(i, i + steps) for i in range(first, last)])


def emit_faces(core, tiles, table_ref, face_refs):
    for index, ref in enumerate(face_refs):
        for b in range(BR):
            if index == 0:
                rows = [tiles[b, 8 * p + 7 * (1 - core)] for p in range(8)]
            elif index == 1:
                rows = [tiles[b, 8 * p + 7 * core] for p in range(8)]
            else:
                rows = [tiles[b, 56 * (index - 2) + q] for q in range(8)]
            ref[64 * b : 64 * b + 64] = jnp.concatenate(rows, axis=0).astype(BF16)
        ref[256:272] = jnp.zeros((16, CH), BF16) if table_ref is None else table_ref[...]


def prep_kernel(core_ref, own_ref, ring1_ref, ring2_ref, ring3_ref, table_ref, tiles_ref, *face_refs):
    for b in range(BR):
        for k in range(4):
            start = OWN * (4 * b + k)
            parts = [ref[start : start + OWN] for ref in (own_ref, ring1_ref, ring2_ref, ring3_ref)]
            turned = jnp.concatenate(parts, axis=0).astype(F32).T
            tiles_ref[b, 16 * k : 16 * k + 16] = turned.reshape(16, 8, CH)
    emit_faces(core_ref[0], tiles_ref, table_ref, face_refs)


def prep(core, blocks, table):
    face = jax.ShapeDtypeStruct((272, CH), BF16)
    return pl.pallas_call(
        prep_kernel,
        out_shape=[jax.ShapeDtypeStruct((BR, 64, 8, CH), F32)] + [face] * 4,
        in_specs=[SMEM] + [VMEM] * 5,
        out_specs=[VMEM] * 5,
        compiler_params=params(6),
        cost_estimate=cost(0, 2**22),
    )(core, *blocks, table)


def turn_kernel(weight_ref, turned_ref):
    blank = jnp.zeros((OWN, CH), BF16)
    for t in range(9):
        block = jnp.concatenate([weight_ref[9 * i + t] for i in range(3)] + [blank], axis=0)
        turned_ref[CH * t : CH * t + CH] = block.astype(F32).T.astype(BF16)


def turn_weight(weight):
    return pl.pallas_call(
        turn_kernel,
        out_shape=jax.ShapeDtypeStruct((9 * CH, CH), BF16),
        in_specs=[VMEM],
        out_specs=VMEM,
        compiler_params=params(4),
        cost_estimate=cost(0, 2**20),
    )(weight)


def turn_field(chan, blocks, start, whole, tiles_ref):
    for step, ref in enumerate(blocks):
        block = lax.rem(chan + 4 - step, 4)
        for k in range(16):
            rows = ref[start + OWN * k : start + OWN * k + OWN]
            whole[pl.ds(pl.multiple_of(block * OWN, OWN), OWN), CH * k : CH * k + CH] = rows.astype(F32)
    for b in range(BR):
        for k in range(4):
            at = VOX * b + CH * k
            tiles_ref[b, 16 * k : 16 * k + 16] = whole[:, at : at + CH].T.reshape(16, 8, CH)


def column(plane, p):
    rows = [plane[64 * b + 8 * p : 64 * b + 8 * p + 8] for b in range(BR)]
    return rows + [plane[256:272]]


def exchange(faces):
    face_m, face_n, low, high = faces
    count = lax.axis_size(SPACE)
    across = [(s, s + 1) for s in range(count) if s % 4 == 1] + [(s, s - 1) for s in range(count) if s % 4 == 2]
    side_n = lax.ppermute(face_n, SPACE, across)
    side_m = lax.ppermute(face_m, "core", [(0, 1), (1, 0)])
    up = jnp.concatenate([high] + column(side_m, 7) + column(side_n, 7), axis=0)
    down = jnp.concatenate([low] + column(side_m, 0) + column(side_n, 0), axis=0)
    return side_m, side_n, shifted(up, ROWS), shifted(down, -ROWS)


def pool_index(entry, core, halo):
    side_m, side_n, left, right = halo
    tables = {
        SIDE_M: side_m[256:272],
        SIDE_N: side_n[256:272],
        SIDE_L: left[256:272],
        SIDE_R: right[256:272],
        SIDE_LM: left[304:320],
        SIDE_LN: left[352:368],
        SIDE_RM: right[304:320],
        SIDE_RN: right[352:368],
    }
    tables = {side: table.astype(F32).astype(jnp.int32) for side, table in tables.items()}
    ends = {-1: (SIDE_LM, SIDE_LN), 0: (SIDE_M, SIDE_N), 1: (SIDE_RM, SIDE_RN)}

    def row(side, d):
        return tables[side][7 - d : 8 - d] + side

    found = jnp.where(entry == 0, ZERO, entry - 65)
    for d, (ex, ey) in enumerate(compass):
        if ey == 0:
            values = row(SIDE_L if ex < 0 else SIDE_R, d)
        else:
            near, far = ends[ex] if ey > 0 else ends[ex][::-1]
            values = jnp.where(core == 0, row(near, d), row(far, d))
        for j in range(SLOTS):
            found = jnp.where(entry == 1 + SLOTS * d + j, values[:, j : j + 1], found)
    return jnp.clip(found, 0, ZERO)


def fill_pool(core, pool, tiles_ref, halo_refs):
    side_m, side_n, left, right = halo_refs
    q_m, q_n = 7 * core, 7 * (1 - core)

    def plane(ref, start):
        return ref[start : start + 64].astype(F32).reshape(8, 8, CH)

    for b in range(BR):
        for first in range(0, 64, 8):
            pool[b, first : first + 8] = tiles_ref[b, first : first + 8]
            pool[ZERO, first : first + 8] = jnp.zeros((8, 8, CH), F32)
        for ref, side, q in ((side_m, SIDE_M, q_m), (side_n, SIDE_N, q_n)):
            rows = plane(ref, 64 * b)
            for p in range(8):
                pool[side + b, 8 * p + q] = rows[p]
        pool[SIDE_L + b, 56:64] = plane(left, 64 * b)
        pool[SIDE_R + b, 0:8] = plane(right, 64 * b)
    for ref, sides, p in ((left, (SIDE_LM, SIDE_LN), 7), (right, (SIDE_RM, SIDE_RN), 0)):
        for side, q, start in ((sides[0], q_m, 272), (sides[1], q_n, 320)):
            rows = ref[start : start + 32].astype(F32).reshape(BR, 8, CH)
            for b in range(BR):
                pool[side + b, 8 * p + q] = rows[b]


def three_shifts(entries, pool, p, q):
    row = lax.broadcasted_iota(jnp.int32, (8, CH), 0)
    first, last = row == 0, row == 7
    shifts = ([], [], [])
    for b in range(BR):
        below = pool[entries[b][0], 8 * p + q]
        centre = pool[entries[b][1], 8 * p + q]
        above = pool[entries[b][2], 8 * p + q]
        shifts[0].append(pltpu.roll(jnp.where(last, below, centre), 1, 0))
        shifts[1].append(centre)
        shifts[2].append(pltpu.roll(jnp.where(first, above, centre), 7, 0))
    return [jnp.concatenate(rows, axis=0).astype(BF16) for rows in shifts]


def inner_windows(neighbours_ref, tiles_ref, zero, windows):
    zero[...] = jnp.zeros_like(zero)
    blank = jnp.zeros((10, 32, CH), BF16)
    for k in range(3):
        windows[k, 0] = blank
        windows[k, 9] = blank
        for p in range(1, 9):
            windows[k, p, 0] = blank[0]
            windows[k, p, 9] = blank[0]
    for b in range(BR):
        zero[b] = tiles_ref[b]
    entries = []
    for b in range(BR):
        found = [neighbours_ref[b, 12 + k] for k in range(3)]
        entries.append([jnp.where(e > 64, e - 65, 4) for e in found])

    def body(p, carry):
        for q in range(8):
            for k, rows in enumerate(three_shifts(entries, zero, p, q)):
                windows[k, p + 1, q + 1] = rows
        return carry

    lax.fori_loop(0, 8, body, 0)


def margin_windows(index_ref, pool, ends, strips):
    blank = jnp.zeros((32, CH), BF16)
    for ox in (-1, 0, 1):
        for oy in (-1, 0, 1):
            if ox == 0 and oy == 0:
                continue
            start = 9 * (ox + 1) + 3 * (oy + 1)
            entries = [[index_ref[b, start + k] for k in range(3)] for b in range(BR)]
            for i in range(8):
                p = i if ox == 0 else (7 if ox < 0 else 0)
                q = i if oy == 0 else (7 if oy < 0 else 0)
                for k, rows in enumerate(three_shifts(entries, pool, p, q)):
                    if ox == 0:
                        strips[(oy + 1) // 2, k, p + 1] = rows
                    else:
                        ends[(ox + 1) // 2, k, q + 1 if oy == 0 else (0 if oy < 0 else 9)] = rows
                if ox != 0 and oy != 0:
                    break
    for side in range(2):
        for k in range(3):
            strips[side, k, 0] = blank
            strips[side, k, 9] = blank


def conv_sum(pairs):
    total = None
    for first in range(0, len(pairs), 2):
        group = pairs[first : first + 2]
        left = jnp.concatenate([rows for rows, _ in group], axis=1)
        right = jnp.concatenate([tap for _, tap in group], axis=0)
        term = jnp.dot(left, right, preferred_element_type=F32)
        total = term if total is None else total + term
    return total


def margin_sums(ends, strips, summed, tap_weight, sign):
    added = []
    for side in range(2):
        along_x, along_y = [], []
        for t in range(TAPS):
            ox, oy, oz = (sign * (v - 1) for v in (t // 9, t // 3 % 3, t % 3))
            if ox == 2 * side - 1:
                along_x.append((ends[side, oz + 1, oy + 1 : oy + 9].reshape(256, CH), tap_weight(t)))
            if oy == 2 * side - 1:
                along_y.append((strips[side, oz + 1, ox + 1 : ox + 9].reshape(256, CH), tap_weight(t)))
        added.append((summed(along_x), summed(along_y)))
    return added


def picks():
    lane = lax.broadcasted_iota(jnp.int32, (CH, CH), 1)
    channel = lax.broadcasted_iota(jnp.int32, (CH, CH), 0)
    parts = [
        jnp.where((lane - OWN * k == channel) & (channel < OWN), 1.0, 0.0).astype(BF16) for k in range(3)
    ]
    return jnp.concatenate(parts, axis=0)


def narrowed(rows, picked):
    return jnp.dot(jnp.concatenate(rows, axis=1), picked, preferred_element_type=F32).astype(BF16)


def inner_kernel(
    nb_ref, chan_ref, tiles_ref, w0_ref, w1_ref, w2_ref, w3_ref, hidden_ref, narrow_ref, cot_ref, zero, windows, wide, padded, whole
):
    inner_windows(nb_ref, tiles_ref, zero, windows)
    blocks = (w0_ref, w1_ref, w2_ref, w3_ref)
    for t in range(TAPS):
        row, lane = CH * (t % 9), CH * (t // 9)
        for s, ref in enumerate(blocks):
            wide[row + OWN * s : row + OWN * s + OWN, lane : lane + CH] = ref[OWN * t : OWN * t + OWN]
    for p in range(10):
        padded[p] = jnp.zeros((8, 32, CH), F32)
    picked = picks()

    def body(p, carry):
        left = [windows[t % 3, p + 1, t // 3 : t // 3 + 8].reshape(256, CH) for t in range(9)]
        total = jnp.dot(jnp.concatenate(left, axis=1), wide[...], preferred_element_type=F32)
        for i in range(3):
            padded[p + 2 - i] += total[:, CH * i : CH * i + CH].reshape(8, 32, CH)
        rows = [windows[k, p + 1, 1:9].reshape(256, CH) for k in range(3)]
        narrow_ref[p] = narrowed(rows, picked).reshape(8, 32, CH)
        return carry

    lax.fori_loop(0, 8, body, 0)
    for p in range(8):
        hidden_ref[p] = padded[p + 1]
    turn_field(chan_ref[0], blocks, TAPS * OWN, whole, cot_ref)


def inner(neighbours, chan, tiles, blocks):
    return pl.pallas_call(
        inner_kernel,
        out_shape=[
            jax.ShapeDtypeStruct((8, 8, 32, CH), F32),
            jax.ShapeDtypeStruct((8, 8, 32, CH), BF16),
            jax.ShapeDtypeStruct((BR, 64, 8, CH), F32),
        ],
        in_specs=[SMEM] * 2 + [VMEM] * 5,
        out_specs=[VMEM] * 3,
        scratch_shapes=[
            pltpu.VMEM((5, 64, 8, CH), F32),
            pltpu.VMEM((3, 10, 10, 32, CH), BF16),
            pltpu.VMEM((9 * CH, 3 * CH), BF16),
            pltpu.VMEM((10, 8, 32, CH), F32),
            pltpu.VMEM((CH, BR * VOX), F32),
        ],
        compiler_params=params(20),
        cost_estimate=cost(2 * 27 * CH * CH * 2048, 2**24),
    )(neighbours, chan, tiles, *blocks)


def gate_kernel(
    place_ref,
    entry_ref,
    tiles_ref,
    cot_ref,
    inner_ref,
    inner_narrow_ref,
    side_m_ref,
    side_n_ref,
    left_ref,
    right_ref,
    w0_ref,
    w1_ref,
    w2_ref,
    w3_ref,
    gated_ref,
    grad_ref,
    face_m_ref,
    face_n_ref,
    low_ref,
    high_ref,
    keep_ref,
    send_ref,
    index_out_ref,
    index_ref,
    pool,
    ends,
    strips,
    hidden,
    narrow,
    grad_rows,
    sums,
):
    core = place_ref[0]
    index_out_ref[...] = pool_index(entry_ref[...], core, (side_m_ref, side_n_ref, left_ref, right_ref))
    pltpu.sync_copy(index_out_ref, index_ref)
    weights = (w0_ref, w1_ref, w2_ref, w3_ref)
    picked = picks()
    fill_pool(core, pool, tiles_ref, (side_m_ref, side_n_ref, left_ref, right_ref))
    margin_windows(index_ref, pool, ends, strips)

    def tap_weight(t):
        return jnp.concatenate([ref[OWN * t : OWN * t + OWN] for ref in weights], axis=0)

    for p in range(8):
        hidden[p] = inner_ref[p]
        narrow[p + 1, 1:9] = inner_narrow_ref[p]
    for side, (along_x, along_y) in enumerate(margin_sums(ends, strips, conv_sum, tap_weight, 1)):
        hidden[7 * side] += along_x.reshape(8, 32, CH)
        for p in range(8):
            hidden[p, 7 * side] += along_y[32 * p : 32 * p + 32]
        rows = [ends[side, k].reshape(320, CH) for k in range(3)]
        narrow[9 * side] = narrowed(rows, picked).reshape(10, 32, CH)
        rows = [strips[side, k, 1:9].reshape(256, CH) for k in range(3)]
        small = narrowed(rows, picked)
        for p in range(8):
            narrow[p + 1, 9 * side] = small[32 * p : 32 * p + 32]

    def gate_body(p, carry):
        h = hidden[p].reshape(8, BR, 8, CH)
        grads = []
        for b in range(BR):
            part = h[:, b]
            cot = cot_ref[b, pl.ds(8 * p, 8)]
            sig = jax.nn.sigmoid(part)
            gated_ref[b, pl.ds(8 * p, 8)] = part * sig
            grad = (cot * sig * (1.0 + part * (1.0 - sig))).astype(BF16).astype(F32)
            grad_ref[b, pl.ds(8 * p, 8)] = grad
            grads.append(grad)
        rows = jnp.stack(grads, axis=1).reshape(256, CH)
        for k in range(2):
            grad_rows[p, :, 128 * k : 128 * k + 128] = rows[128 * k : 128 * k + 128].T.astype(BF16)
        return carry

    lax.fori_loop(0, 8, gate_body, 0)
    emit_faces(core, grad_ref, None, (face_m_ref, face_n_ref, low_ref, high_ref))

    left = jnp.concatenate([grad_rows[p] for p in range(8)], axis=1)
    for first in range(0, 9, 2):
        group = range(first, min(first + 2, 9))
        right = [narrow[t // 3 : t // 3 + 8, t % 3 : t % 3 + 8].reshape(2048, CH) for t in group]
        total = jnp.dot(left, jnp.concatenate(right, axis=1), preferred_element_type=F32)
        for k, t in enumerate(group):
            sums[96 * t : 96 * t + 96] = total[:, CH * k : CH * k + CH].T[:96]
    sums[864:896] = jnp.zeros((32, CH), F32)
    keep_ref[...] = sums[pl.ds(pl.multiple_of(448 * core, 8), 448), :]
    send_ref[...] = sums[pl.ds(pl.multiple_of(448 * (1 - core), 8), 448), :]


def gate(core, entries, tiles, cot, hidden, narrow, halo, weights):
    face = jax.ShapeDtypeStruct((272, CH), BF16)
    half = jax.ShapeDtypeStruct((448, CH), F32)
    field = jax.ShapeDtypeStruct((BR, 64, 8, CH), F32)
    return pl.pallas_call(
        gate_kernel,
        out_shape=[field, field, face, face, face, face, half, half, jax.ShapeDtypeStruct((8, CH), jnp.int32)],
        in_specs=[SMEM] + [VMEM] * 13,
        out_specs=[VMEM] * 9,
        scratch_shapes=[
            pltpu.SMEM((8, CH), jnp.int32),
            pltpu.VMEM((40, 64, 8, CH), F32),
            pltpu.VMEM((2, 3, 10, 32, CH), BF16),
            pltpu.VMEM((2, 3, 10, 32, CH), BF16),
            pltpu.VMEM((8, 8, 32, CH), F32),
            pltpu.VMEM((10, 10, 32, CH), BF16),
            pltpu.VMEM((8, CH, 256), BF16),
            pltpu.VMEM((896, CH), F32),
        ],
        compiler_params=params(28),
        cost_estimate=cost(2 * 27 * CH * CH * 1024, 2**24),
    )(core, entries, tiles, cot, hidden, narrow, *halo, *weights)


def back_inner_kernel(nb_ref, tiles_ref, turned_ref, part_ref, zero, windows, planes):
    inner_windows(nb_ref, tiles_ref, zero, windows)
    planes[0] = jnp.zeros((256, CH), F32)
    planes[9] = jnp.zeros((256, CH), F32)

    def body(p, carry):
        left = [windows[2 - t % 3, p + 1, 2 - t // 3 : 10 - t // 3].reshape(256, CH) for t in range(9)]
        planes[p + 1] = jnp.dot(jnp.concatenate(left, axis=1), turned_ref[...], preferred_element_type=F32)
        return carry

    lax.fori_loop(0, 8, body, 0)
    for p in range(8):
        summed = planes[p + 2] + pltpu.roll(planes[p + 1], CH - OWN, 1) + pltpu.roll(planes[p], CH - 2 * OWN, 1)
        part_ref[p] = summed.reshape(8, 32, CH)


def back_inner(neighbours, tiles, turned):
    return pl.pallas_call(
        back_inner_kernel,
        out_shape=jax.ShapeDtypeStruct((8, 8, 32, CH), F32),
        in_specs=[SMEM] + [VMEM] * 2,
        out_specs=VMEM,
        scratch_shapes=[
            pltpu.VMEM((5, 64, 8, CH), F32),
            pltpu.VMEM((3, 10, 10, 32, CH), BF16),
            pltpu.VMEM((10, 256, CH), F32),
        ],
        compiler_params=params(14),
        cost_estimate=cost(2 * 27 * CH * CH * 1024, 2**23),
    )(neighbours, tiles, turned)


def output_kernel(chan_ref, gated_ref, feat_ref, out_ref, turned):
    own = pl.multiple_of(chan_ref[0] * OWN, OWN)
    for k in range(16):
        turned[k] = gated_ref[k // 4, 16 * (k % 4) : 16 * (k % 4) + 16].reshape(128, CH).T
        rows = feat_ref[OWN * k : OWN * k + OWN].astype(F32) + turned[k, pl.ds(own, OWN), :]
        out_ref[OWN * k : OWN * k + OWN] = rows.astype(BF16)


def output_of(chan, gated, features):
    return pl.pallas_call(
        output_kernel,
        out_shape=jax.ShapeDtypeStruct((16 * OWN, CH), BF16),
        in_specs=[SMEM] + [VMEM] * 2,
        out_specs=VMEM,
        scratch_shapes=[pltpu.VMEM((16, CH, CH), F32)],
        compiler_params=params(6),
        cost_estimate=cost(0, 2**22),
    )(chan, gated, features)


def back_margin_kernel(
    place_ref,
    index_in_ref,
    tiles_ref,
    side_m_ref,
    side_n_ref,
    left_ref,
    right_ref,
    turned_ref,
    part_ref,
    cot_ref,
    grad_ref,
    index_ref,
    pool,
    ends,
    strips,
    result,
):
    pltpu.sync_copy(index_in_ref, index_ref)
    fill_pool(place_ref[0], pool, tiles_ref, (side_m_ref, side_n_ref, left_ref, right_ref))
    margin_windows(index_ref, pool, ends, strips)
    for p in range(8):
        result[p] = part_ref[p]
    blank = jnp.zeros((32, CH), F32)
    for side in range(2):
        left = [ends[side, 2 - t % 3, 2 - t // 3 : 10 - t // 3].reshape(256, CH) for t in range(9)]
        along_x = jnp.dot(jnp.concatenate(left, axis=1), turned_ref[...], preferred_element_type=F32)
        if side == 0:
            along_x = pltpu.roll(along_x, CH - 2 * OWN, 1)
        result[7 * side] += along_x.reshape(8, 32, CH)
        j = 2 - 2 * side
        left = [strips[side, 2 - k, 1:9].reshape(256, CH) for k in range(3)]
        along_y = jnp.dot(
            jnp.concatenate(left, axis=1), turned_ref[3 * CH * j : 3 * CH * (j + 1)], preferred_element_type=F32
        )
        here = pltpu.roll(along_y, CH - OWN, 1)
        before = pltpu.roll(along_y, CH - 2 * OWN, 1)
        for p in range(8):
            rows = here[32 * p : 32 * p + 32]
            if p < 7:
                rows = rows + along_y[32 * p + 32 : 32 * p + 64]
            if p > 0:
                rows = rows + before[32 * p - 32 : 32 * p]
            result[p, 7 * side] += rows
    for b in range(BR):
        for k in range(4):
            at = OWN * (4 * b + k)
            block = result[2 * k : 2 * k + 2, :, 8 * b : 8 * b + 8, :].reshape(128, CH)
            summed = cot_ref[at : at + OWN].astype(F32) + block.T[:OWN]
            grad_ref[at : at + OWN] = summed.astype(BF16)


def back_margin(core, index, tiles, halo, turned, part, cotangent):
    return pl.pallas_call(
        back_margin_kernel,
        out_shape=jax.ShapeDtypeStruct((16 * OWN, CH), BF16),
        in_specs=[SMEM] + [VMEM] * 9,
        out_specs=VMEM,
        scratch_shapes=[
            pltpu.SMEM((8, CH), jnp.int32),
            pltpu.VMEM((40, 64, 8, CH), F32),
            pltpu.VMEM((2, 3, 10, 32, CH), BF16),
            pltpu.VMEM((2, 3, 10, 32, CH), BF16),
            pltpu.VMEM((8, 8, 32, CH), F32),
        ],
        compiler_params=params(20),
        cost_estimate=cost(2 * 27 * CH * CH * 512, 2**23),
    )(core, index, tiles, *halo, turned, part, cotangent)


def ring_gather(value, axis):
    count = lax.axis_size(axis)
    blocks = [value]
    for step in range(1, count):
        blocks.append(lax.ppermute(value, axis, [(i, (i + step) % count) for i in range(count)]))
    return blocks


def swapped(value, axis, partner):
    return lax.ppermute(value, axis, list(enumerate(partner)))


X_NEAR, X_FAR = (1, 0, 3, 2), (3, 2, 1, 0)
Z_PAIRS = ((1, 0, 3, 2, 5, 4, 7, 6), (2, 3, 0, 1, 6, 7, 4, 5), (6, 7, 4, 5, 2, 3, 0, 1))


def halve(value, bit, partner):
    halves = value.reshape(2, value.shape[0] // 2, CH)
    keep = lax.dynamic_index_in_dim(halves, bit, 0, keepdims=False)
    send = lax.dynamic_index_in_dim(halves, 1 - bit, 0, keepdims=False)
    return keep + swapped(send, "x", partner)


def place_kernel(me_ref, one_ref, two_ref, four_ref, eight_ref, out_ref):
    for t in range(8):
        if t < 1:
            rows = one_ref[...]
        elif t < 2:
            rows = two_ref[...]
        elif t < 4:
            rows = four_ref[112 * (t - 2) : 112 * (t - 1)]
        else:
            rows = eight_ref[112 * (t - 4) : 112 * (t - 3)]
        at = me_ref[t]
        start = pl.multiple_of(112 * at, 8)

        @pl.when(at < 7)
        def _():
            out_ref[pl.ds(start, 112), :] = rows

        @pl.when(at == 7)
        def _():
            out_ref[pl.ds(start, 80), :] = rows[:80]


def after(value, *others):
    return lax.optimization_barrier((value,) + others)[0]


def reduce_space(keep, send, beside):
    x = lax.axis_index("x")
    core = lax.axis_index("core")
    high = x // 2
    low = (x ^ (x // 2)) & 1
    value = keep + swapped(send, "core", (1, 0))
    value = halve(value, high, X_FAR)
    value = halve(after(value, *beside[0]), low, X_NEAR)
    for step, partner in enumerate(Z_PAIRS):
        value = after(value, *beside[step + 1])
        value = value + swapped(value, "z", partner)
    value = after(value, *beside[4])
    two = swapped(value, "x", X_NEAR)
    pair = jnp.concatenate([value, two], axis=0)
    four = swapped(pair, "x", X_FAR)
    quad = jnp.concatenate([pair, four], axis=0)
    eight = swapped(quad, "core", (1, 0))
    me = 4 * core + 2 * high + low
    return pl.pallas_call(
        place_kernel,
        out_shape=jax.ShapeDtypeStruct((864, CH), F32),
        in_specs=[SMEM] + [VMEM] * 4,
        out_specs=VMEM,
        compiler_params=params(4),
        cost_estimate=cost(0, 2**20),
    )(me ^ jnp.arange(8, dtype=jnp.int32), value, two, four, eight)


def to_rows(field):
    return field.reshape(OWN, 16, CH).transpose(1, 0, 2).reshape(16 * OWN, CH)


def from_rows(rows):
    return rows.reshape(16, OWN, CH).transpose(1, 0, 2).reshape(OWN, BR, VOX)


def per_device(features, weight, cotangent, neighbours, send_slots):
    core = lax.axis_index("core").astype(jnp.int32).reshape(1)
    chan = lax.axis_index("chan").astype(jnp.int32).reshape(1)
    feat_own = to_rows(features)
    cot_own = to_rows(cotangent)
    table = jnp.pad(send_slots.astype(BF16), ((0, 8), (0, CH - SLOTS)))
    entries = jnp.pad(neighbours, ((0, 4), (0, CH - TAPS)))
    feat_blocks = ring_gather(feat_own, "chan")
    both = jnp.concatenate([weight.reshape(TAPS * OWN, CH), cot_own], axis=0)
    blocks = ring_gather(both, "chan")
    turned = turn_weight(weight)
    table = after(table, turned, entries)

    tiles, *faces = prep(core, feat_blocks, table)
    halo = exchange(faces)
    hidden, narrow, cot = inner(neighbours, chan, tiles, blocks)
    gated, grads, *rest = gate(core, entries, tiles, cot, hidden, narrow, halo, blocks)
    grad_faces, keep, send, index = rest[:4], rest[4], rest[5], rest[6]
    grad_halo = exchange(grad_faces)
    part = back_inner(neighbours, grads, turned)
    out = output_of(chan, gated, feat_own)
    grad_input = back_margin(core, index, grads, grad_halo, turned, part, cot_own)
    grad_weight = reduce_space(keep, send, ((part,), (out,), (), (grad_input,), ()))
    return (from_rows(out), from_rows(grad_input), grad_weight.reshape(TAPS, OWN, CH))


def solution(mesh):
    fine = Mesh(mesh.devices.reshape(4, 8, 2, 4), ("x", "z", "core", "chan"))
    return jax.shard_map(
        per_device,
        mesh=fine,
        in_specs=(
            P("chan", SPACE, None),
            P(None, "chan", None),
            P("chan", SPACE, None),
            P(SPACE, None),
            P(SPACE, None),
        ),
        out_specs=(P("chan", SPACE, None), P("chan", SPACE, None), P(None, "chan", None)),
        check_vma=False,
    )
```

```python
import jax
import jax.numpy as jnp
from jax import lax
from jax.experimental import pallas as pl
from jax.experimental.pallas import tpu as pltpu
from jax.sharding import Mesh, PartitionSpec as P

ROWS = 4
CH = 128
OWN = 32
BR = 4
VOX = 512
TAPS = 27
SLOTS = 8
F32 = jnp.float32
BF16 = jnp.bfloat16
SPACE = ("x", "z", "core")
VMEM = pl.BlockSpec(memory_space=pltpu.VMEM)
SMEM = pl.BlockSpec(memory_space=pltpu.SMEM)

compass = ((-1, -1), (-1, 0), (-1, 1), (0, -1), (0, 1), (1, -1), (1, 0), (1, 1))
SIDE_M, SIDE_N, SIDE_L, SIDE_R, SIDE_LM, SIDE_LN, SIDE_RM, SIDE_RN, ZERO = range(4, 40, 4)


def params(mib):
    return pltpu.CompilerParams(vmem_limit_bytes=mib * 2**20)


def cost(flops, moved):
    return pl.CostEstimate(flops=flops, bytes_accessed=moved, transcendentals=0)


def shifted(value, steps):
    count = lax.axis_size(SPACE)
    first, last = max(0, -steps), min(count, count - steps)
    return lax.ppermute(value, SPACE, [(i, i + steps) for i in range(first, last)])


def emit_faces(core, tiles, table_ref, face_refs):
    for index, ref in enumerate(face_refs):
        for b in range(BR):
            if index == 0:
                rows = [tiles[b, 8 * p + 7 * (1 - core)] for p in range(8)]
            elif index == 1:
                rows = [tiles[b, 8 * p + 7 * core] for p in range(8)]
            else:
                rows = [tiles[b, 56 * (index - 2) + q] for q in range(8)]
            ref[64 * b : 64 * b + 64] = jnp.concatenate(rows, axis=0).astype(BF16)
        ref[256:272] = jnp.zeros((16, CH), BF16) if table_ref is None else table_ref[...]


def prep_kernel(core_ref, own_ref, ring1_ref, ring2_ref, ring3_ref, table_ref, tiles_ref, *face_refs):
    for b in range(BR):
        for k in range(4):
            start = OWN * (4 * b + k)
            parts = [ref[start : start + OWN] for ref in (own_ref, ring1_ref, ring2_ref, ring3_ref)]
            turned = jnp.concatenate(parts, axis=0).astype(F32).T
            tiles_ref[b, 16 * k : 16 * k + 16] = turned.reshape(16, 8, CH)
    emit_faces(core_ref[0], tiles_ref, table_ref, face_refs)


def prep(core, blocks, table):
    face = jax.ShapeDtypeStruct((272, CH), BF16)
    return pl.pallas_call(
        prep_kernel,
        out_shape=[jax.ShapeDtypeStruct((BR, 64, 8, CH), F32)] + [face] * 4,
        in_specs=[SMEM] + [VMEM] * 5,
        out_specs=[VMEM] * 5,
        compiler_params=params(4),
        cost_estimate=cost(0, 2**22),
    )(core, *blocks, table)


def turn_kernel(weight_ref, turned_ref):
    blank = jnp.zeros((OWN, CH), BF16)
    for t in range(9):
        block = jnp.concatenate([weight_ref[9 * i + t] for i in range(3)] + [blank], axis=0)
        turned_ref[CH * t : CH * t + CH] = block.astype(F32).T.astype(BF16)


def turn_weight(weight):
    return pl.pallas_call(
        turn_kernel,
        out_shape=jax.ShapeDtypeStruct((9 * CH, CH), BF16),
        in_specs=[VMEM],
        out_specs=VMEM,
        compiler_params=params(2),
        cost_estimate=cost(0, 2**20),
    )(weight)


def turn_field(chan, blocks, start, whole, tiles_ref):
    for step, ref in enumerate(blocks):
        block = lax.rem(chan + 4 - step, 4)
        for k in range(16):
            rows = ref[start + OWN * k : start + OWN * k + OWN]
            whole[pl.ds(pl.multiple_of(block * OWN, OWN), OWN), CH * k : CH * k + CH] = rows.astype(F32)
    for b in range(BR):
        for k in range(4):
            at = VOX * b + CH * k
            tiles_ref[b, 16 * k : 16 * k + 16] = whole[:, at : at + CH].T.reshape(16, 8, CH)


def column(plane, p):
    rows = [plane[64 * b + 8 * p : 64 * b + 8 * p + 8] for b in range(BR)]
    return rows + [plane[256:272]]


def exchange(faces):
    face_m, face_n, low, high = faces
    count = lax.axis_size(SPACE)
    across = [(s, s + 1) for s in range(count) if s % 4 == 1] + [(s, s - 1) for s in range(count) if s % 4 == 2]
    side_n = lax.ppermute(face_n, SPACE, across)
    side_m = lax.ppermute(face_m, "core", [(0, 1), (1, 0)])
    up = jnp.concatenate([high] + column(side_m, 7) + column(side_n, 7), axis=0)
    down = jnp.concatenate([low] + column(side_m, 0) + column(side_n, 0), axis=0)
    return side_m, side_n, shifted(up, ROWS), shifted(down, -ROWS)


def pool_index(entry, core, halo):
    side_m, side_n, left, right = halo
    tables = {
        SIDE_M: side_m[256:272],
        SIDE_N: side_n[256:272],
        SIDE_L: left[256:272],
        SIDE_R: right[256:272],
        SIDE_LM: left[304:320],
        SIDE_LN: left[352:368],
        SIDE_RM: right[304:320],
        SIDE_RN: right[352:368],
    }
    tables = {side: table.astype(F32).astype(jnp.int32) for side, table in tables.items()}
    ends = {-1: (SIDE_LM, SIDE_LN), 0: (SIDE_M, SIDE_N), 1: (SIDE_RM, SIDE_RN)}

    def row(side, d):
        return tables[side][7 - d : 8 - d] + side

    found = jnp.where(entry == 0, ZERO, entry - 65)
    for d, (ex, ey) in enumerate(compass):
        if ey == 0:
            values = row(SIDE_L if ex < 0 else SIDE_R, d)
        else:
            near, far = ends[ex] if ey > 0 else ends[ex][::-1]
            values = jnp.where(core == 0, row(near, d), row(far, d))
        for j in range(SLOTS):
            found = jnp.where(entry == 1 + SLOTS * d + j, values[:, j : j + 1], found)
    return jnp.clip(found, 0, ZERO)


P_HIGH, P_LOW, Q_HIGH, Q_LOW = range(4)


def fill_pool(core, pool, tiles_ref, halo_refs):
    side_m, side_n, left, right = halo_refs
    q_m, q_n = 7 * core, 7 * (1 - core)

    def plane(ref, start):
        return ref[start : start + 64].astype(F32).reshape(8, 8, CH)

    for m in range(4):
        pool[m, ZERO] = jnp.zeros((8, 8, CH), F32)
    for b in range(BR):
        pool[P_HIGH, b] = tiles_ref[b, 56:64]
        pool[P_LOW, b] = tiles_ref[b, 0:8]
        for p in range(8):
            pool[Q_HIGH, b, p] = tiles_ref[b, 8 * p + 7]
            pool[Q_LOW, b, p] = tiles_ref[b, 8 * p]
        for ref, side, q in ((side_m, SIDE_M, q_m), (side_n, SIDE_N, q_n)):
            rows = plane(ref, 64 * b)
            pool[Q_HIGH, side + b] = rows
            pool[Q_LOW, side + b] = rows
            pool[P_HIGH, side + b, q] = rows[7]
            pool[P_LOW, side + b, q] = rows[0]
        pool[P_HIGH, SIDE_L + b] = plane(left, 64 * b)
        pool[P_LOW, SIDE_R + b] = plane(right, 64 * b)
    for ref, sides, m in ((left, (SIDE_LM, SIDE_LN), P_HIGH), (right, (SIDE_RM, SIDE_RN), P_LOW)):
        for side, q, start in ((sides[0], q_m, 272), (sides[1], q_n, 320)):
            rows = ref[start : start + 32].astype(F32).reshape(BR, 8, CH)
            for b in range(BR):
                pool[m, side + b, q] = rows[b]


def three_shifts(entries, tile):
    row = lax.broadcasted_iota(jnp.int32, (8, CH), 0)
    first, last = row == 0, row == 7
    shifts = ([], [], [])
    for b in range(BR):
        below = tile(entries[b][0])
        centre = tile(entries[b][1])
        above = tile(entries[b][2])
        shifts[0].append(pltpu.roll(jnp.where(last, below, centre), 1, 0))
        shifts[1].append(centre)
        shifts[2].append(pltpu.roll(jnp.where(first, above, centre), 7, 0))
    return [jnp.concatenate(rows, axis=0).astype(BF16) for rows in shifts]


def inner_windows(neighbours_ref, tiles_ref, zero, windows):
    zero[...] = jnp.zeros_like(zero)
    blank = jnp.zeros((10, 32, CH), BF16)
    for k in range(3):
        windows[k, 0] = blank
        windows[k, 9] = blank
        for p in range(1, 9):
            windows[k, p, 0] = blank[0]
            windows[k, p, 9] = blank[0]
    for b in range(BR):
        zero[b] = tiles_ref[b]
    entries = []
    for b in range(BR):
        found = [neighbours_ref[b, 12 + k] for k in range(3)]
        entries.append([jnp.where(e > 64, e - 65, 4) for e in found])

    def body(p, carry):
        for q in range(8):
            for k, rows in enumerate(three_shifts(entries, lambda e: zero[e, 8 * p + q])):
                windows[k, p + 1, q + 1] = rows
        return carry

    lax.fori_loop(0, 8, body, 0)


def margin_windows(index_ref, pool, ends, strips):
    blank = jnp.zeros((32, CH), BF16)
    for ox in (-1, 0, 1):
        for oy in (-1, 0, 1):
            if ox == 0 and oy == 0:
                continue
            start = 9 * (ox + 1) + 3 * (oy + 1)
            entries = [[index_ref[b, start + k] for k in range(3)] for b in range(BR)]
            if ox == 0:
                m = Q_HIGH if oy < 0 else Q_LOW
            else:
                m = P_HIGH if ox < 0 else P_LOW
            corner = ox != 0 and oy != 0
            for i in ((7 if oy < 0 else 0),) if corner else range(8):
                for k, rows in enumerate(three_shifts(entries, lambda e: pool[m, e, i])):
                    if ox == 0:
                        strips[(oy + 1) // 2, k, i + 1] = rows
                    else:
                        ends[(ox + 1) // 2, k, i + 1 if not corner else (0 if oy < 0 else 9)] = rows
    for side in range(2):
        for k in range(3):
            strips[side, k, 0] = blank
            strips[side, k, 9] = blank


def conv_sum(pairs):
    total = None
    for first in range(0, len(pairs), 2):
        group = pairs[first : first + 2]
        left = jnp.concatenate([rows for rows, _ in group], axis=1)
        right = jnp.concatenate([tap for _, tap in group], axis=0)
        term = jnp.dot(left, right, preferred_element_type=F32)
        total = term if total is None else total + term
    return total


def margin_sums(ends, strips, summed, tap_weight, sign):
    added = []
    for side in range(2):
        along_x, along_y = [], []
        for t in range(TAPS):
            ox, oy, oz = (sign * (v - 1) for v in (t // 9, t // 3 % 3, t % 3))
            if ox == 2 * side - 1:
                along_x.append((ends[side, oz + 1, oy + 1 : oy + 9].reshape(256, CH), tap_weight(t)))
            if oy == 2 * side - 1:
                along_y.append((strips[side, oz + 1, ox + 1 : ox + 9].reshape(256, CH), tap_weight(t)))
        added.append((summed(along_x), summed(along_y)))
    return added


def picks():
    lane = lax.broadcasted_iota(jnp.int32, (CH, CH), 1)
    channel = lax.broadcasted_iota(jnp.int32, (CH, CH), 0)
    parts = [
        jnp.where((lane - OWN * k == channel) & (channel < OWN), 1.0, 0.0).astype(BF16) for k in range(3)
    ]
    return jnp.concatenate(parts, axis=0)


def narrowed(rows, picked):
    return jnp.dot(jnp.concatenate(rows, axis=1), picked, preferred_element_type=F32).astype(BF16)


def inner_kernel(
    nb_ref, chan_ref, tiles_ref, w0_ref, w1_ref, w2_ref, w3_ref, hidden_ref, narrow_ref, cot_ref, zero, windows, wide, padded, whole
):
    inner_windows(nb_ref, tiles_ref, zero, windows)
    blocks = (w0_ref, w1_ref, w2_ref, w3_ref)
    for t in range(TAPS):
        row, lane = CH * (t % 9), CH * (t // 9)
        for s, ref in enumerate(blocks):
            wide[row + OWN * s : row + OWN * s + OWN, lane : lane + CH] = ref[OWN * t : OWN * t + OWN]
    for p in range(10):
        padded[p] = jnp.zeros((8, 32, CH), F32)
    picked = picks()

    def body(p, carry):
        left = [windows[t % 3, p + 1, t // 3 : t // 3 + 8].reshape(256, CH) for t in range(9)]
        total = jnp.dot(jnp.concatenate(left, axis=1), wide[...], preferred_element_type=F32)
        for i in range(3):
            padded[p + 2 - i] += total[:, CH * i : CH * i + CH].reshape(8, 32, CH)
        rows = [windows[k, p + 1, 1:9].reshape(256, CH) for k in range(3)]
        narrow_ref[p] = narrowed(rows, picked).reshape(8, 32, CH)
        return carry

    lax.fori_loop(0, 8, body, 0)
    for p in range(8):
        hidden_ref[p] = padded[p + 1]
    turn_field(chan_ref[0], blocks, TAPS * OWN, whole, cot_ref)


def inner(neighbours, chan, tiles, blocks):
    return pl.pallas_call(
        inner_kernel,
        out_shape=[
            jax.ShapeDtypeStruct((8, 8, 32, CH), F32),
            jax.ShapeDtypeStruct((8, 8, 32, CH), BF16),
            jax.ShapeDtypeStruct((BR, 64, 8, CH), F32),
        ],
        in_specs=[SMEM] * 2 + [VMEM] * 5,
        out_specs=[VMEM] * 3,
        scratch_shapes=[
            pltpu.VMEM((5, 64, 8, CH), F32),
            pltpu.VMEM((3, 10, 10, 32, CH), BF16),
            pltpu.VMEM((9 * CH, 3 * CH), BF16),
            pltpu.VMEM((10, 8, 32, CH), F32),
            pltpu.VMEM((CH, BR * VOX), F32),
        ],
        compiler_params=params(13),
        cost_estimate=cost(2 * 27 * CH * CH * 2048, 2**24),
    )(neighbours, chan, tiles, *blocks)


def gate_kernel(
    place_ref,
    entry_ref,
    tiles_ref,
    cot_ref,
    inner_ref,
    inner_narrow_ref,
    side_m_ref,
    side_n_ref,
    left_ref,
    right_ref,
    w0_ref,
    w1_ref,
    w2_ref,
    w3_ref,
    gated_ref,
    grad_ref,
    face_m_ref,
    face_n_ref,
    low_ref,
    high_ref,
    keep_ref,
    send_ref,
    index_out_ref,
    index_ref,
    pool,
    ends,
    strips,
    hidden,
    narrow,
    grad_rows,
    sums,
):
    core = place_ref[0]
    index_out_ref[...] = pool_index(entry_ref[...], core, (side_m_ref, side_n_ref, left_ref, right_ref))
    pltpu.sync_copy(index_out_ref, index_ref)
    weights = (w0_ref, w1_ref, w2_ref, w3_ref)
    picked = picks()
    fill_pool(core, pool, tiles_ref, (side_m_ref, side_n_ref, left_ref, right_ref))
    margin_windows(index_ref, pool, ends, strips)

    def tap_weight(t):
        return jnp.concatenate([ref[OWN * t : OWN * t + OWN] for ref in weights], axis=0)

    for p in range(8):
        hidden[p] = inner_ref[p]
        narrow[p + 1, 1:9] = inner_narrow_ref[p]
    for side, (along_x, along_y) in enumerate(margin_sums(ends, strips, conv_sum, tap_weight, 1)):
        hidden[7 * side] += along_x.reshape(8, 32, CH)
        for p in range(8):
            hidden[p, 7 * side] += along_y[32 * p : 32 * p + 32]
        rows = [ends[side, k].reshape(320, CH) for k in range(3)]
        narrow[9 * side] = narrowed(rows, picked).reshape(10, 32, CH)
        rows = [strips[side, k, 1:9].reshape(256, CH) for k in range(3)]
        small = narrowed(rows, picked)
        for p in range(8):
            narrow[p + 1, 9 * side] = small[32 * p : 32 * p + 32]

    def gate_body(p, carry):
        h = hidden[p].reshape(8, BR, 8, CH)
        grads = []
        for b in range(BR):
            part = h[:, b]
            cot = cot_ref[b, pl.ds(8 * p, 8)]
            sig = jax.nn.sigmoid(part)
            gated_ref[b, pl.ds(8 * p, 8)] = part * sig
            grad = (cot * sig * (1.0 + part * (1.0 - sig))).astype(BF16).astype(F32)
            grad_ref[b, pl.ds(8 * p, 8)] = grad
            grads.append(grad)
        rows = jnp.stack(grads, axis=1).reshape(256, CH)
        for k in range(2):
            grad_rows[p, :, 128 * k : 128 * k + 128] = rows[128 * k : 128 * k + 128].T.astype(BF16)
        return carry

    lax.fori_loop(0, 8, gate_body, 0)
    emit_faces(core, grad_ref, None, (face_m_ref, face_n_ref, low_ref, high_ref))

    left = jnp.concatenate([grad_rows[p] for p in range(8)], axis=1)
    for first in range(0, 9, 2):
        group = range(first, min(first + 2, 9))
        right = [narrow[t // 3 : t // 3 + 8, t % 3 : t % 3 + 8].reshape(2048, CH) for t in group]
        total = jnp.dot(left, jnp.concatenate(right, axis=1), preferred_element_type=F32)
        for k, t in enumerate(group):
            sums[96 * t : 96 * t + 96] = total[:, CH * k : CH * k + CH].T[:96]
    sums[864:896] = jnp.zeros((32, CH), F32)
    keep_ref[...] = sums[pl.ds(pl.multiple_of(448 * core, 8), 448), :]
    send_ref[...] = sums[pl.ds(pl.multiple_of(448 * (1 - core), 8), 448), :]


def gate(core, entries, tiles, cot, hidden, narrow, halo, weights):
    face = jax.ShapeDtypeStruct((272, CH), BF16)
    half = jax.ShapeDtypeStruct((448, CH), F32)
    field = jax.ShapeDtypeStruct((BR, 64, 8, CH), F32)
    return pl.pallas_call(
        gate_kernel,
        out_shape=[field, field, face, face, face, face, half, half, jax.ShapeDtypeStruct((8, CH), jnp.int32)],
        in_specs=[SMEM] + [VMEM] * 13,
        out_specs=[VMEM] * 9,
        scratch_shapes=[
            pltpu.SMEM((8, CH), jnp.int32),
            pltpu.VMEM((4, 40, 8, 8, CH), F32),
            pltpu.VMEM((2, 3, 10, 32, CH), BF16),
            pltpu.VMEM((2, 3, 10, 32, CH), BF16),
            pltpu.VMEM((8, 8, 32, CH), F32),
            pltpu.VMEM((10, 10, 32, CH), BF16),
            pltpu.VMEM((8, CH, 256), BF16),
            pltpu.VMEM((896, CH), F32),
        ],
        compiler_params=params(18),
        cost_estimate=cost(2 * 27 * CH * CH * 1024, 2**24),
    )(core, entries, tiles, cot, hidden, narrow, *halo, *weights)


def back_inner_kernel(nb_ref, tiles_ref, turned_ref, part_ref, zero, windows, planes):
    inner_windows(nb_ref, tiles_ref, zero, windows)
    planes[0] = jnp.zeros((256, CH), F32)
    planes[9] = jnp.zeros((256, CH), F32)

    def body(p, carry):
        left = [windows[2 - t % 3, p + 1, 2 - t // 3 : 10 - t // 3].reshape(256, CH) for t in range(9)]
        planes[p + 1] = jnp.dot(jnp.concatenate(left, axis=1), turned_ref[...], preferred_element_type=F32)
        return carry

    lax.fori_loop(0, 8, body, 0)
    for p in range(8):
        summed = planes[p + 2] + pltpu.roll(planes[p + 1], CH - OWN, 1) + pltpu.roll(planes[p], CH - 2 * OWN, 1)
        part_ref[p] = summed.reshape(8, 32, CH)


def back_inner(neighbours, tiles, turned):
    return pl.pallas_call(
        back_inner_kernel,
        out_shape=jax.ShapeDtypeStruct((8, 8, 32, CH), F32),
        in_specs=[SMEM] + [VMEM] * 2,
        out_specs=VMEM,
        scratch_shapes=[
            pltpu.VMEM((5, 64, 8, CH), F32),
            pltpu.VMEM((3, 10, 10, 32, CH), BF16),
            pltpu.VMEM((10, 256, CH), F32),
        ],
        compiler_params=params(8),
        cost_estimate=cost(2 * 27 * CH * CH * 1024, 2**23),
    )(neighbours, tiles, turned)


def output_kernel(chan_ref, gated_ref, feat_ref, out_ref, turned):
    own = pl.multiple_of(chan_ref[0] * OWN, OWN)
    for k in range(16):
        turned[k] = gated_ref[k // 4, 16 * (k % 4) : 16 * (k % 4) + 16].reshape(128, CH).T
        rows = feat_ref[OWN * k : OWN * k + OWN].astype(F32) + turned[k, pl.ds(own, OWN), :]
        out_ref[OWN * k : OWN * k + OWN] = rows.astype(BF16)


def output_of(chan, gated, features):
    return pl.pallas_call(
        output_kernel,
        out_shape=jax.ShapeDtypeStruct((16 * OWN, CH), BF16),
        in_specs=[SMEM] + [VMEM] * 2,
        out_specs=VMEM,
        scratch_shapes=[pltpu.VMEM((16, CH, CH), F32)],
        compiler_params=params(4),
        cost_estimate=cost(0, 2**22),
    )(chan, gated, features)


def back_margin_kernel(
    place_ref,
    index_in_ref,
    tiles_ref,
    side_m_ref,
    side_n_ref,
    left_ref,
    right_ref,
    turned_ref,
    part_ref,
    cot_ref,
    grad_ref,
    index_ref,
    pool,
    ends,
    strips,
    result,
):
    pltpu.sync_copy(index_in_ref, index_ref)
    fill_pool(place_ref[0], pool, tiles_ref, (side_m_ref, side_n_ref, left_ref, right_ref))
    margin_windows(index_ref, pool, ends, strips)
    for p in range(8):
        result[p] = part_ref[p]
    blank = jnp.zeros((32, CH), F32)
    for side in range(2):
        left = [ends[side, 2 - t % 3, 2 - t // 3 : 10 - t // 3].reshape(256, CH) for t in range(9)]
        along_x = jnp.dot(jnp.concatenate(left, axis=1), turned_ref[...], preferred_element_type=F32)
        if side == 0:
            along_x = pltpu.roll(along_x, CH - 2 * OWN, 1)
        result[7 * side] += along_x.reshape(8, 32, CH)
        j = 2 - 2 * side
        left = [strips[side, 2 - k, 1:9].reshape(256, CH) for k in range(3)]
        along_y = jnp.dot(
            jnp.concatenate(left, axis=1), turned_ref[3 * CH * j : 3 * CH * (j + 1)], preferred_element_type=F32
        )
        here = pltpu.roll(along_y, CH - OWN, 1)
        before = pltpu.roll(along_y, CH - 2 * OWN, 1)
        for p in range(8):
            rows = here[32 * p : 32 * p + 32]
            if p < 7:
                rows = rows + along_y[32 * p + 32 : 32 * p + 64]
            if p > 0:
                rows = rows + before[32 * p - 32 : 32 * p]
            result[p, 7 * side] += rows
    for b in range(BR):
        for k in range(4):
            at = OWN * (4 * b + k)
            block = result[2 * k : 2 * k + 2, :, 8 * b : 8 * b + 8, :].reshape(128, CH)
            summed = cot_ref[at : at + OWN].astype(F32) + block.T[:OWN]
            grad_ref[at : at + OWN] = summed.astype(BF16)


def back_margin(core, index, tiles, halo, turned, part, cotangent):
    return pl.pallas_call(
        back_margin_kernel,
        out_shape=jax.ShapeDtypeStruct((16 * OWN, CH), BF16),
        in_specs=[SMEM] + [VMEM] * 9,
        out_specs=VMEM,
        scratch_shapes=[
            pltpu.SMEM((8, CH), jnp.int32),
            pltpu.VMEM((4, 40, 8, 8, CH), F32),
            pltpu.VMEM((2, 3, 10, 32, CH), BF16),
            pltpu.VMEM((2, 3, 10, 32, CH), BF16),
            pltpu.VMEM((8, 8, 32, CH), F32),
        ],
        compiler_params=params(12),
        cost_estimate=cost(2 * 27 * CH * CH * 512, 2**23),
    )(core, index, tiles, *halo, turned, part, cotangent)


def ring_gather(value, axis):
    count = lax.axis_size(axis)
    blocks = [value]
    for step in range(1, count):
        blocks.append(lax.ppermute(value, axis, [(i, (i + step) % count) for i in range(count)]))
    return blocks


def swapped(value, axis, partner):
    return lax.ppermute(value, axis, list(enumerate(partner)))


X_PARTNERS = ((1, 0, 3, 2), (3, 2, 1, 0), (2, 3, 0, 1))
Z_PAIRS = ((1, 0, 3, 2, 5, 4, 7, 6), (2, 3, 0, 1, 6, 7, 4, 5), (6, 7, 4, 5, 2, 3, 0, 1))


def place_kernel(me_ref, one_ref, two_ref, four_ref, eight_ref, out_ref):
    for t in range(8):
        if t < 1:
            rows = one_ref[...]
        elif t < 2:
            rows = two_ref[...]
        elif t < 4:
            rows = four_ref[112 * (t - 2) : 112 * (t - 1)]
        else:
            rows = eight_ref[112 * (t - 4) : 112 * (t - 3)]
        at = me_ref[t]
        start = pl.multiple_of(112 * at, 8)

        @pl.when(at < 7)
        def _():
            out_ref[pl.ds(start, 112), :] = rows

        @pl.when(at == 7)
        def _():
            out_ref[pl.ds(start, 80), :] = rows[:80]


def after(value, *others):
    return lax.optimization_barrier((value,) + others)[0]


def reduce_space(keep, send, work):
    x = lax.axis_index("x")
    core = lax.axis_index("core")
    label = x ^ (x // 2)

    def beside(step, value, got):
        return after(got, *work[step](value)) if step in work else got

    def halve(value, bit, partner):
        halves = value.reshape(2, value.shape[0] // 2, CH)
        kept = lax.dynamic_index_in_dim(halves, bit, 0, keepdims=False)
        sent = lax.dynamic_index_in_dim(halves, 1 - bit, 0, keepdims=False)
        return kept + swapped(sent, "x", partner)

    value = keep + swapped(send, "core", (1, 0))
    value = halve(value, label // 2, X_PARTNERS[1])
    value = halve(value, label % 2, X_PARTNERS[0])
    for step, partner in enumerate(Z_PAIRS):
        value = value + beside(step, value, swapped(value, "z", partner))
    others = [swapped(value, "x", partner) for partner in X_PARTNERS]
    others[0] = beside(3, value, others[0])
    quad = jnp.concatenate([value] + others, axis=0)
    eight = swapped(quad, "core", (1, 0))
    me = 4 * core + label
    two = others[0]
    four = jnp.concatenate(others[1:], axis=0)
    return pl.pallas_call(
        place_kernel,
        out_shape=jax.ShapeDtypeStruct((864, CH), F32),
        in_specs=[SMEM] + [VMEM] * 4,
        out_specs=VMEM,
        compiler_params=params(3),
        cost_estimate=cost(0, 2**20),
    )(me ^ jnp.arange(8, dtype=jnp.int32), value, two, four, eight)


def to_rows(field):
    return field.reshape(OWN, 16, CH).transpose(1, 0, 2).reshape(16 * OWN, CH)


def from_rows(rows):
    return rows.reshape(16, OWN, CH).transpose(1, 0, 2).reshape(OWN, BR, VOX)


def per_device(features, weight, cotangent, neighbours, send_slots):
    core = lax.axis_index("core").astype(jnp.int32).reshape(1)
    chan = lax.axis_index("chan").astype(jnp.int32).reshape(1)
    feat_own = to_rows(features)
    cot_own = to_rows(cotangent)
    table = jnp.pad(send_slots.astype(BF16), ((0, 8), (0, CH - SLOTS)))
    entries = jnp.pad(neighbours, ((0, 4), (0, CH - TAPS)))
    feat_blocks = ring_gather(feat_own, "chan")
    both = jnp.concatenate([weight.reshape(TAPS * OWN, CH), cot_own], axis=0)
    blocks = ring_gather(both, "chan")
    turned = turn_weight(weight)
    table = after(table, turned, entries)

    tiles, *faces = prep(core, feat_blocks, table)
    halo = exchange(faces)
    hidden, narrow, cot = inner(neighbours, chan, tiles, blocks)
    gated, grads, *rest = gate(core, entries, tiles, cot, hidden, narrow, halo, blocks)
    grad_faces, keep, send, index = rest[:4], rest[4], rest[5], rest[6]
    grad_halo = exchange(grad_faces)
    made = {}

    def inner_part(value):
        made["part"] = back_inner(after(neighbours, value[:8]), grads, turned)
        return (made["part"],)

    def margin_part(value):
        here = after(core, value[:8])
        made["grad"] = from_rows(back_margin(here, index, grads, grad_halo, turned, made["part"], cot_own))
        return (made["grad"],)

    def output_part(value):
        made["out"] = from_rows(output_of(after(chan, value[:8]), gated, feat_own))
        return (made["out"],)

    work = {0: inner_part, 2: margin_part, 3: output_part}
    grad_weight = reduce_space(keep, send, work)
    out, grad_input = made["out"], made["grad"]
    return (out, grad_input, grad_weight.reshape(TAPS, OWN, CH))


def solution(mesh):
    fine = Mesh(mesh.devices.reshape(4, 8, 2, 4), ("x", "z", "core", "chan"))
    return jax.shard_map(
        per_device,
        mesh=fine,
        in_specs=(
            P("chan", SPACE, None),
            P(None, "chan", None),
            P("chan", SPACE, None),
            P(SPACE, None),
            P(SPACE, None),
        ),
        out_specs=(P("chan", SPACE, None), P("chan", SPACE, None), P(None, "chan", None)),
        check_vma=False,
    )
```

```python
import jax
import jax.numpy as jnp
from jax import lax
from jax.experimental import pallas as pl
from jax.experimental.pallas import tpu as pltpu
from jax.sharding import Mesh, PartitionSpec as P

ROWS = 4
CH = 128
OWN = 32
BR = 4
VOX = 512
TAPS = 27
SLOTS = 8
F32 = jnp.float32
BF16 = jnp.bfloat16
SPACE = ("x", "z", "core")
VMEM = pl.BlockSpec(memory_space=pltpu.VMEM)
SMEM = pl.BlockSpec(memory_space=pltpu.SMEM)

compass = ((-1, -1), (-1, 0), (-1, 1), (0, -1), (0, 1), (1, -1), (1, 0), (1, 1))
SIDE_M, SIDE_N, SIDE_L, SIDE_R, SIDE_LM, SIDE_LN, SIDE_RM, SIDE_RN, ZERO = range(4, 40, 4)


def params(mib):
    return pltpu.CompilerParams(vmem_limit_bytes=mib * 2**20)


def cost(flops, moved):
    return pl.CostEstimate(flops=flops, bytes_accessed=moved, transcendentals=0)


def shifted(value, steps):
    count = lax.axis_size(SPACE)
    first, last = max(0, -steps), min(count, count - steps)
    return lax.ppermute(value, SPACE, [(i, i + steps) for i in range(first, last)])


def emit_faces(core, tiles, table_ref, face_refs):
    for index, ref in enumerate(face_refs):
        for b in range(BR):
            if index == 0:
                rows = [tiles[b, 8 * p + 7 * (1 - core)] for p in range(8)]
            elif index == 1:
                rows = [tiles[b, 8 * p + 7 * core] for p in range(8)]
            else:
                rows = [tiles[b, 56 * (index - 2) + q] for q in range(8)]
            ref[64 * b : 64 * b + 64] = jnp.concatenate(rows, axis=0).astype(BF16)
        ref[256:272] = jnp.zeros((16, CH), BF16) if table_ref is None else table_ref[...]


def prep_kernel(core_ref, own_ref, ring1_ref, ring2_ref, ring3_ref, table_ref, tiles_ref, *face_refs):
    for b in range(BR):
        for k in range(4):
            start = OWN * (4 * b + k)
            parts = [ref[start : start + OWN] for ref in (own_ref, ring1_ref, ring2_ref, ring3_ref)]
            turned = jnp.concatenate(parts, axis=0).astype(F32).T
            tiles_ref[b, 16 * k : 16 * k + 16] = turned.reshape(16, 8, CH)
    emit_faces(core_ref[0], tiles_ref, table_ref, face_refs)


def prep(core, blocks, table):
    face = jax.ShapeDtypeStruct((272, CH), BF16)
    return pl.pallas_call(
        prep_kernel,
        out_shape=[jax.ShapeDtypeStruct((BR, 64, 8, CH), F32)] + [face] * 4,
        in_specs=[SMEM] + [VMEM] * 5,
        out_specs=[VMEM] * 5,
        compiler_params=params(4),
        cost_estimate=cost(0, 2**22),
    )(core, *blocks, table)


def turn_kernel(weight_ref, turned_ref):
    blank = jnp.zeros((OWN, CH), BF16)
    for t in range(9):
        block = jnp.concatenate([weight_ref[9 * i + t] for i in range(3)] + [blank], axis=0)
        turned_ref[CH * t : CH * t + CH] = block.astype(F32).T.astype(BF16)


def turn_weight(weight):
    return pl.pallas_call(
        turn_kernel,
        out_shape=jax.ShapeDtypeStruct((9 * CH, CH), BF16),
        in_specs=[VMEM],
        out_specs=VMEM,
        compiler_params=params(2),
        cost_estimate=cost(0, 2**20),
    )(weight)


def turn_field(chan, blocks, start, whole, tiles_ref):
    for step, ref in enumerate(blocks):
        block = lax.rem(chan + 4 - step, 4)
        for k in range(16):
            rows = ref[start + OWN * k : start + OWN * k + OWN]
            whole[pl.ds(pl.multiple_of(block * OWN, OWN), OWN), CH * k : CH * k + CH] = rows.astype(F32)
    for b in range(BR):
        for k in range(4):
            at = VOX * b + CH * k
            tiles_ref[b, 16 * k : 16 * k + 16] = whole[:, at : at + CH].T.reshape(16, 8, CH)


def column(plane, p):
    rows = [plane[64 * b + 8 * p : 64 * b + 8 * p + 8] for b in range(BR)]
    return rows + [plane[256:272]]


def exchange(faces):
    face_m, face_n, low, high = faces
    count = lax.axis_size(SPACE)
    across = [(s, s + 1) for s in range(count) if s % 4 == 1] + [(s, s - 1) for s in range(count) if s % 4 == 2]
    side_n = lax.ppermute(face_n, SPACE, across)
    side_m = lax.ppermute(face_m, "core", [(0, 1), (1, 0)])
    up = jnp.concatenate([high] + column(side_m, 7) + column(side_n, 7), axis=0)
    down = jnp.concatenate([low] + column(side_m, 0) + column(side_n, 0), axis=0)
    return side_m, side_n, shifted(up, ROWS), shifted(down, -ROWS)


def pool_index(entry, core, halo):
    side_m, side_n, left, right = halo
    tables = {
        SIDE_M: side_m[256:272],
        SIDE_N: side_n[256:272],
        SIDE_L: left[256:272],
        SIDE_R: right[256:272],
        SIDE_LM: left[304:320],
        SIDE_LN: left[352:368],
        SIDE_RM: right[304:320],
        SIDE_RN: right[352:368],
    }
    tables = {side: table.astype(F32).astype(jnp.int32) for side, table in tables.items()}
    ends = {-1: (SIDE_LM, SIDE_LN), 0: (SIDE_M, SIDE_N), 1: (SIDE_RM, SIDE_RN)}

    def row(side, d):
        return tables[side][7 - d : 8 - d] + side

    found = jnp.where(entry == 0, ZERO, entry - 65)
    for d, (ex, ey) in enumerate(compass):
        if ey == 0:
            values = row(SIDE_L if ex < 0 else SIDE_R, d)
        else:
            near, far = ends[ex] if ey > 0 else ends[ex][::-1]
            values = jnp.where(core == 0, row(near, d), row(far, d))
        for j in range(SLOTS):
            found = jnp.where(entry == 1 + SLOTS * d + j, values[:, j : j + 1], found)
    return jnp.clip(found, 0, ZERO)


P_HIGH, P_LOW, Q_HIGH, Q_LOW = range(4)


def fill_pool(core, pool, tiles_ref, halo_refs):
    side_m, side_n, left, right = halo_refs
    q_m, q_n = 7 * core, 7 * (1 - core)

    def plane(ref, start):
        return ref[start : start + 64].astype(F32).reshape(8, 8, CH)

    for m in range(4):
        pool[m, ZERO] = jnp.zeros((8, 8, CH), F32)
    for b in range(BR):
        pool[P_HIGH, b] = tiles_ref[b, 56:64]
        pool[P_LOW, b] = tiles_ref[b, 0:8]
        for p in range(8):
            pool[Q_HIGH, b, p] = tiles_ref[b, 8 * p + 7]
            pool[Q_LOW, b, p] = tiles_ref[b, 8 * p]
        for ref, side, q in ((side_m, SIDE_M, q_m), (side_n, SIDE_N, q_n)):
            rows = plane(ref, 64 * b)
            pool[Q_HIGH, side + b] = rows
            pool[Q_LOW, side + b] = rows
            pool[P_HIGH, side + b, q] = rows[7]
            pool[P_LOW, side + b, q] = rows[0]
        pool[P_HIGH, SIDE_L + b] = plane(left, 64 * b)
        pool[P_LOW, SIDE_R + b] = plane(right, 64 * b)
    for ref, sides, m in ((left, (SIDE_LM, SIDE_LN), P_HIGH), (right, (SIDE_RM, SIDE_RN), P_LOW)):
        for side, q, start in ((sides[0], q_m, 272), (sides[1], q_n, 320)):
            rows = ref[start : start + 32].astype(F32).reshape(BR, 8, CH)
            for b in range(BR):
                pool[m, side + b, q] = rows[b]


def three_shifts(entries, tile):
    row = lax.broadcasted_iota(jnp.int32, (8, CH), 0)
    first, last = row == 0, row == 7
    shifts = ([], [], [])
    for b in range(BR):
        below = tile(entries[b][0])
        centre = tile(entries[b][1])
        above = tile(entries[b][2])
        shifts[0].append(pltpu.roll(jnp.where(last, below, centre), 1, 0))
        shifts[1].append(centre)
        shifts[2].append(pltpu.roll(jnp.where(first, above, centre), 7, 0))
    return [jnp.concatenate(rows, axis=0).astype(BF16) for rows in shifts]


def inner_windows(neighbours_ref, tiles_ref, zero, windows):
    zero[...] = jnp.zeros_like(zero)
    blank = jnp.zeros((10, 32, CH), BF16)
    for k in range(3):
        windows[k, 0] = blank
        windows[k, 9] = blank
        for p in range(1, 9):
            windows[k, p, 0] = blank[0]
            windows[k, p, 9] = blank[0]
    for b in range(BR):
        zero[b] = tiles_ref[b]
    entries = []
    for b in range(BR):
        found = [neighbours_ref[b, 12 + k] for k in range(3)]
        entries.append([jnp.where(e > 64, e - 65, 4) for e in found])

    def body(p, carry):
        for q in range(8):
            for k, rows in enumerate(three_shifts(entries, lambda e: zero[e, 8 * p + q])):
                windows[k, p + 1, q + 1] = rows
        return carry

    lax.fori_loop(0, 8, body, 0)


def margin_windows(index_ref, pool, ends, strips):
    blank = jnp.zeros((32, CH), BF16)
    for ox in (-1, 0, 1):
        for oy in (-1, 0, 1):
            if ox == 0 and oy == 0:
                continue
            start = 9 * (ox + 1) + 3 * (oy + 1)
            entries = [[index_ref[b, start + k] for k in range(3)] for b in range(BR)]
            if ox == 0:
                m = Q_HIGH if oy < 0 else Q_LOW
            else:
                m = P_HIGH if ox < 0 else P_LOW
            corner = ox != 0 and oy != 0
            for i in ((7 if oy < 0 else 0),) if corner else range(8):
                for k, rows in enumerate(three_shifts(entries, lambda e: pool[m, e, i])):
                    if ox == 0:
                        strips[(oy + 1) // 2, k, i + 1] = rows
                    else:
                        ends[(ox + 1) // 2, k, i + 1 if not corner else (0 if oy < 0 else 9)] = rows
    for side in range(2):
        for k in range(3):
            strips[side, k, 0] = blank
            strips[side, k, 9] = blank


def conv_sum(pairs):
    total = None
    for first in range(0, len(pairs), 2):
        group = pairs[first : first + 2]
        left = jnp.concatenate([rows for rows, _ in group], axis=1)
        right = jnp.concatenate([tap for _, tap in group], axis=0)
        term = jnp.dot(left, right, preferred_element_type=F32)
        total = term if total is None else total + term
    return total


def margin_sums(ends, strips, summed, tap_weight, sign):
    added = []
    for side in range(2):
        along_x, along_y = [], []
        for t in range(TAPS):
            ox, oy, oz = (sign * (v - 1) for v in (t // 9, t // 3 % 3, t % 3))
            if ox == 2 * side - 1:
                along_x.append((ends[side, oz + 1, oy + 1 : oy + 9].reshape(256, CH), tap_weight(t)))
            if oy == 2 * side - 1:
                along_y.append((strips[side, oz + 1, ox + 1 : ox + 9].reshape(256, CH), tap_weight(t)))
        added.append((summed(along_x), summed(along_y)))
    return added


def picks():
    lane = lax.broadcasted_iota(jnp.int32, (CH, CH), 1)
    channel = lax.broadcasted_iota(jnp.int32, (CH, CH), 0)
    parts = [
        jnp.where((lane - OWN * k == channel) & (channel < OWN), 1.0, 0.0).astype(BF16) for k in range(3)
    ]
    return jnp.concatenate(parts, axis=0)


def narrowed(rows, picked):
    return jnp.dot(jnp.concatenate(rows, axis=1), picked, preferred_element_type=F32).astype(BF16)


def inner_kernel(
    nb_ref, chan_ref, tiles_ref, w0_ref, w1_ref, w2_ref, w3_ref, hidden_ref, narrow_ref, cot_ref, zero, windows, wide, padded, whole
):
    inner_windows(nb_ref, tiles_ref, zero, windows)
    blocks = (w0_ref, w1_ref, w2_ref, w3_ref)
    for t in range(TAPS):
        row, lane = CH * (t % 9), CH * (t // 9)
        for s, ref in enumerate(blocks):
            wide[row + OWN * s : row + OWN * s + OWN, lane : lane + CH] = ref[OWN * t : OWN * t + OWN]
    for p in range(10):
        padded[p] = jnp.zeros((8, 32, CH), F32)
    picked = picks()

    def body(p, carry):
        left = [windows[t % 3, p + 1, t // 3 : t // 3 + 8].reshape(256, CH) for t in range(9)]
        total = jnp.dot(jnp.concatenate(left, axis=1), wide[...], preferred_element_type=F32)
        for i in range(3):
            padded[p + 2 - i] += total[:, CH * i : CH * i + CH].reshape(8, 32, CH)
        rows = [windows[k, p + 1, 1:9].reshape(256, CH) for k in range(3)]
        narrow_ref[p] = narrowed(rows, picked).reshape(8, 32, CH)
        return carry

    lax.fori_loop(0, 8, body, 0)
    for p in range(8):
        hidden_ref[p] = padded[p + 1]
    turn_field(chan_ref[0], blocks, TAPS * OWN, whole, cot_ref)


def inner(neighbours, chan, tiles, blocks):
    return pl.pallas_call(
        inner_kernel,
        out_shape=[
            jax.ShapeDtypeStruct((8, 8, 32, CH), F32),
            jax.ShapeDtypeStruct((8, 8, 32, CH), BF16),
            jax.ShapeDtypeStruct((BR, 64, 8, CH), F32),
        ],
        in_specs=[SMEM] * 2 + [VMEM] * 5,
        out_specs=[VMEM] * 3,
        scratch_shapes=[
            pltpu.VMEM((5, 64, 8, CH), F32),
            pltpu.VMEM((3, 10, 10, 32, CH), BF16),
            pltpu.VMEM((9 * CH, 3 * CH), BF16),
            pltpu.VMEM((10, 8, 32, CH), F32),
            pltpu.VMEM((CH, BR * VOX), F32),
        ],
        compiler_params=params(13),
        cost_estimate=cost(2 * 27 * CH * CH * 2048, 2**24),
    )(neighbours, chan, tiles, *blocks)


def gate_kernel(
    place_ref,
    entry_ref,
    tiles_ref,
    cot_ref,
    inner_ref,
    inner_narrow_ref,
    side_m_ref,
    side_n_ref,
    left_ref,
    right_ref,
    w0_ref,
    w1_ref,
    w2_ref,
    w3_ref,
    gated_ref,
    grad_ref,
    face_m_ref,
    face_n_ref,
    low_ref,
    high_ref,
    keep_ref,
    send_ref,
    index_out_ref,
    index_ref,
    pool,
    ends,
    strips,
    hidden,
    narrow,
    grad_rows,
    sums,
):
    core = place_ref[0]
    index_out_ref[...] = pool_index(entry_ref[...], core, (side_m_ref, side_n_ref, left_ref, right_ref))
    pltpu.sync_copy(index_out_ref, index_ref)
    weights = (w0_ref, w1_ref, w2_ref, w3_ref)
    picked = picks()
    fill_pool(core, pool, tiles_ref, (side_m_ref, side_n_ref, left_ref, right_ref))
    margin_windows(index_ref, pool, ends, strips)

    def tap_weight(t):
        return jnp.concatenate([ref[OWN * t : OWN * t + OWN] for ref in weights], axis=0)

    for p in range(8):
        hidden[p] = inner_ref[p]
        narrow[p + 1, 1:9] = inner_narrow_ref[p]
    for side, (along_x, along_y) in enumerate(margin_sums(ends, strips, conv_sum, tap_weight, 1)):
        hidden[7 * side] += along_x.reshape(8, 32, CH)
        for p in range(8):
            hidden[p, 7 * side] += along_y[32 * p : 32 * p + 32]
        rows = [ends[side, k].reshape(320, CH) for k in range(3)]
        narrow[9 * side] = narrowed(rows, picked).reshape(10, 32, CH)
        rows = [strips[side, k, 1:9].reshape(256, CH) for k in range(3)]
        small = narrowed(rows, picked)
        for p in range(8):
            narrow[p + 1, 9 * side] = small[32 * p : 32 * p + 32]

    def gate_body(p, carry):
        h = hidden[p].reshape(8, BR, 8, CH)
        grads = []
        for b in range(BR):
            part = h[:, b]
            cot = cot_ref[b, pl.ds(8 * p, 8)]
            sig = jax.nn.sigmoid(part)
            gated_ref[b, pl.ds(8 * p, 8)] = part * sig
            grad = (cot * sig * (1.0 + part * (1.0 - sig))).astype(BF16).astype(F32)
            grad_ref[b, pl.ds(8 * p, 8)] = grad
            grads.append(grad)
        rows = jnp.stack(grads, axis=1).reshape(256, CH)
        for k in range(2):
            grad_rows[p, :, 128 * k : 128 * k + 128] = rows[128 * k : 128 * k + 128].T.astype(BF16)
        return carry

    lax.fori_loop(0, 8, gate_body, 0)
    emit_faces(core, grad_ref, None, (face_m_ref, face_n_ref, low_ref, high_ref))

    left = jnp.concatenate([grad_rows[p] for p in range(8)], axis=1)
    for first in range(0, 9, 2):
        group = range(first, min(first + 2, 9))
        right = [narrow[t // 3 : t // 3 + 8, t % 3 : t % 3 + 8].reshape(2048, CH) for t in group]
        total = jnp.dot(left, jnp.concatenate(right, axis=1), preferred_element_type=F32)
        for k, t in enumerate(group):
            sums[96 * t : 96 * t + 96] = total[:, CH * k : CH * k + CH].T[:96]
    sums[864:896] = jnp.zeros((32, CH), F32)
    keep_ref[...] = sums[pl.ds(pl.multiple_of(448 * core, 8), 448), :]
    send_ref[...] = sums[pl.ds(pl.multiple_of(448 * (1 - core), 8), 448), :]


def gate(core, entries, tiles, cot, hidden, narrow, halo, weights):
    face = jax.ShapeDtypeStruct((272, CH), BF16)
    half = jax.ShapeDtypeStruct((448, CH), F32)
    field = jax.ShapeDtypeStruct((BR, 64, 8, CH), F32)
    return pl.pallas_call(
        gate_kernel,
        out_shape=[field, field, face, face, face, face, half, half, jax.ShapeDtypeStruct((8, CH), jnp.int32)],
        in_specs=[SMEM] + [VMEM] * 13,
        out_specs=[VMEM] * 9,
        scratch_shapes=[
            pltpu.SMEM((8, CH), jnp.int32),
            pltpu.VMEM((4, 40, 8, 8, CH), F32),
            pltpu.VMEM((2, 3, 10, 32, CH), BF16),
            pltpu.VMEM((2, 3, 10, 32, CH), BF16),
            pltpu.VMEM((8, 8, 32, CH), F32),
            pltpu.VMEM((10, 10, 32, CH), BF16),
            pltpu.VMEM((8, CH, 256), BF16),
            pltpu.VMEM((896, CH), F32),
        ],
        compiler_params=params(18),
        cost_estimate=cost(2 * 27 * CH * CH * 1024, 2**24),
    )(core, entries, tiles, cot, hidden, narrow, *halo, *weights)


def back_inner_kernel(nb_ref, tiles_ref, turned_ref, part_ref, zero, windows, planes):
    inner_windows(nb_ref, tiles_ref, zero, windows)
    planes[0] = jnp.zeros((256, CH), F32)
    planes[9] = jnp.zeros((256, CH), F32)

    def body(p, carry):
        left = [windows[2 - t % 3, p + 1, 2 - t // 3 : 10 - t // 3].reshape(256, CH) for t in range(9)]
        planes[p + 1] = jnp.dot(jnp.concatenate(left, axis=1), turned_ref[...], preferred_element_type=F32)
        return carry

    lax.fori_loop(0, 8, body, 0)
    for p in range(8):
        summed = planes[p + 2] + pltpu.roll(planes[p + 1], CH - OWN, 1) + pltpu.roll(planes[p], CH - 2 * OWN, 1)
        part_ref[p] = summed.reshape(8, 32, CH)


def back_inner(neighbours, tiles, turned):
    return pl.pallas_call(
        back_inner_kernel,
        out_shape=jax.ShapeDtypeStruct((8, 8, 32, CH), F32),
        in_specs=[SMEM] + [VMEM] * 2,
        out_specs=VMEM,
        scratch_shapes=[
            pltpu.VMEM((5, 64, 8, CH), F32),
            pltpu.VMEM((3, 10, 10, 32, CH), BF16),
            pltpu.VMEM((10, 256, CH), F32),
        ],
        compiler_params=params(8),
        cost_estimate=cost(2 * 27 * CH * CH * 1024, 2**23),
    )(neighbours, tiles, turned)


def output_kernel(chan_ref, gated_ref, feat_ref, out_ref, turned):
    own = pl.multiple_of(chan_ref[0] * OWN, OWN)
    for k in range(16):
        turned[k] = gated_ref[k // 4, 16 * (k % 4) : 16 * (k % 4) + 16].reshape(128, CH).T
        rows = feat_ref[OWN * k : OWN * k + OWN].astype(F32) + turned[k, pl.ds(own, OWN), :]
        out_ref[OWN * k : OWN * k + OWN] = rows.astype(BF16)


def output_of(chan, gated, features):
    return pl.pallas_call(
        output_kernel,
        out_shape=jax.ShapeDtypeStruct((16 * OWN, CH), BF16),
        in_specs=[SMEM] + [VMEM] * 2,
        out_specs=VMEM,
        scratch_shapes=[pltpu.VMEM((16, CH, CH), F32)],
        compiler_params=params(4),
        cost_estimate=cost(0, 2**22),
    )(chan, gated, features)


def back_margin_kernel(
    place_ref,
    index_in_ref,
    tiles_ref,
    side_m_ref,
    side_n_ref,
    left_ref,
    right_ref,
    turned_ref,
    part_ref,
    cot_ref,
    grad_ref,
    index_ref,
    pool,
    ends,
    strips,
    result,
):
    pltpu.sync_copy(index_in_ref, index_ref)
    fill_pool(place_ref[0], pool, tiles_ref, (side_m_ref, side_n_ref, left_ref, right_ref))
    margin_windows(index_ref, pool, ends, strips)
    for p in range(8):
        result[p] = part_ref[p]
    blank = jnp.zeros((32, CH), F32)
    for side in range(2):
        left = [ends[side, 2 - t % 3, 2 - t // 3 : 10 - t // 3].reshape(256, CH) for t in range(9)]
        along_x = jnp.dot(jnp.concatenate(left, axis=1), turned_ref[...], preferred_element_type=F32)
        if side == 0:
            along_x = pltpu.roll(along_x, CH - 2 * OWN, 1)
        result[7 * side] += along_x.reshape(8, 32, CH)
        j = 2 - 2 * side
        left = [strips[side, 2 - k, 1:9].reshape(256, CH) for k in range(3)]
        along_y = jnp.dot(
            jnp.concatenate(left, axis=1), turned_ref[3 * CH * j : 3 * CH * (j + 1)], preferred_element_type=F32
        )
        here = pltpu.roll(along_y, CH - OWN, 1)
        before = pltpu.roll(along_y, CH - 2 * OWN, 1)
        for p in range(8):
            rows = here[32 * p : 32 * p + 32]
            if p < 7:
                rows = rows + along_y[32 * p + 32 : 32 * p + 64]
            if p > 0:
                rows = rows + before[32 * p - 32 : 32 * p]
            result[p, 7 * side] += rows
    for b in range(BR):
        for k in range(4):
            at = OWN * (4 * b + k)
            block = result[2 * k : 2 * k + 2, :, 8 * b : 8 * b + 8, :].reshape(128, CH)
            summed = cot_ref[at : at + OWN].astype(F32) + block.T[:OWN]
            grad_ref[at : at + OWN] = summed.astype(BF16)


def back_margin(core, index, tiles, halo, turned, part, cotangent):
    return pl.pallas_call(
        back_margin_kernel,
        out_shape=jax.ShapeDtypeStruct((16 * OWN, CH), BF16),
        in_specs=[SMEM] + [VMEM] * 9,
        out_specs=VMEM,
        scratch_shapes=[
            pltpu.SMEM((8, CH), jnp.int32),
            pltpu.VMEM((4, 40, 8, 8, CH), F32),
            pltpu.VMEM((2, 3, 10, 32, CH), BF16),
            pltpu.VMEM((2, 3, 10, 32, CH), BF16),
            pltpu.VMEM((8, 8, 32, CH), F32),
        ],
        compiler_params=params(12),
        cost_estimate=cost(2 * 27 * CH * CH * 512, 2**23),
    )(core, index, tiles, *halo, turned, part, cotangent)


def ring_gather(value, axis):
    count = lax.axis_size(axis)
    blocks = [value]
    for step in range(1, count):
        blocks.append(lax.ppermute(value, axis, [(i, (i + step) % count) for i in range(count)]))
    return blocks


def swapped(value, axis, partner):
    return lax.ppermute(value, axis, list(enumerate(partner)))


X_PARTNERS = ((1, 0, 3, 2), (3, 2, 1, 0), (2, 3, 0, 1))
Z_PAIRS = tuple(tuple(i ^ mask for i in range(8)) for mask in (6, 1, 2))


def place_kernel(me_ref, one_ref, two_ref, four_ref, eight_ref, out_ref):
    for t in range(8):
        if t < 1:
            rows = one_ref[...]
        elif t < 2:
            rows = two_ref[...]
        elif t < 4:
            rows = four_ref[112 * (t - 2) : 112 * (t - 1)]
        else:
            rows = eight_ref[112 * (t - 4) : 112 * (t - 3)]
        at = me_ref[t]
        start = pl.multiple_of(112 * at, 8)

        @pl.when(at < 7)
        def _():
            out_ref[pl.ds(start, 112), :] = rows

        @pl.when(at == 7)
        def _():
            out_ref[pl.ds(start, 80), :] = rows[:80]


def after(value, *others):
    return lax.optimization_barrier((value,) + others)[0]


def reduce_space(keep, send, work):
    x = lax.axis_index("x")
    core = lax.axis_index("core")
    label = x ^ (x // 2)

    def beside(step, value, got):
        return after(got, *work[step](value)) if step in work else got

    def halve(value, bit, partner):
        halves = value.reshape(2, value.shape[0] // 2, CH)
        kept = lax.dynamic_index_in_dim(halves, bit, 0, keepdims=False)
        sent = lax.dynamic_index_in_dim(halves, 1 - bit, 0, keepdims=False)
        return kept + swapped(sent, "x", partner)

    value = keep + swapped(send, "core", (1, 0))
    value = halve(value, label // 2, X_PARTNERS[1])
    value = halve(value, label % 2, X_PARTNERS[0])
    for step, partner in enumerate(Z_PAIRS):
        value = value + beside(step, value, swapped(value, "z", partner))
    others = [swapped(value, "x", partner) for partner in X_PARTNERS]
    others[0] = beside(3, value, others[0])
    quad = jnp.concatenate([value] + others, axis=0)
    eight = swapped(quad, "core", (1, 0))
    me = 4 * core + label
    two = others[0]
    four = jnp.concatenate(others[1:], axis=0)
    return pl.pallas_call(
        place_kernel,
        out_shape=jax.ShapeDtypeStruct((864, CH), F32),
        in_specs=[SMEM] + [VMEM] * 4,
        out_specs=VMEM,
        compiler_params=params(3),
        cost_estimate=cost(0, 2**20),
    )(me ^ jnp.arange(8, dtype=jnp.int32), value, two, four, eight)


def to_rows(field):
    return field.reshape(OWN, 16, CH).transpose(1, 0, 2).reshape(16 * OWN, CH)


def from_rows(rows):
    return rows.reshape(16, OWN, CH).transpose(1, 0, 2).reshape(OWN, BR, VOX)


def per_device(features, weight, cotangent, neighbours, send_slots):
    core = lax.axis_index("core").astype(jnp.int32).reshape(1)
    chan = lax.axis_index("chan").astype(jnp.int32).reshape(1)
    feat_own = to_rows(features)
    cot_own = to_rows(cotangent)
    table = jnp.pad(send_slots.astype(BF16), ((0, 8), (0, CH - SLOTS)))
    entries = jnp.pad(neighbours, ((0, 4), (0, CH - TAPS)))
    feat_blocks = ring_gather(feat_own, "chan")
    both = jnp.concatenate([weight.reshape(TAPS * OWN, CH), cot_own], axis=0)
    blocks = ring_gather(both, "chan")
    turned = turn_weight(weight)
    table = after(table, turned, entries)

    tiles, *faces = prep(core, feat_blocks, table)
    halo = exchange(faces)
    hidden, narrow, cot = inner(neighbours, chan, tiles, blocks)
    gated, grads, *rest = gate(core, entries, tiles, cot, hidden, narrow, halo, blocks)
    grad_faces, keep, send, index = rest[:4], rest[4], rest[5], rest[6]
    grad_halo = exchange(grad_faces)
    made = {}

    def inner_part(value):
        made["part"] = back_inner(after(neighbours, value[:8]), grads, turned)
        return (made["part"],)

    def margin_part(value):
        here = after(core, value[:8])
        made["grad"] = from_rows(back_margin(here, index, grads, grad_halo, turned, made["part"], cot_own))
        return (made["grad"],)

    def output_part(value):
        made["out"] = from_rows(output_of(after(chan, value[:8]), gated, feat_own))
        return (made["out"],)

    work = {0: inner_part, 2: margin_part, 3: output_part}
    grad_weight = reduce_space(keep, send, work)
    out, grad_input = made["out"], made["grad"]
    return (out, grad_input, grad_weight.reshape(TAPS, OWN, CH))


def solution(mesh):
    fine = Mesh(mesh.devices.reshape(4, 8, 2, 4), ("x", "z", "core", "chan"))
    return jax.shard_map(
        per_device,
        mesh=fine,
        in_specs=(
            P("chan", SPACE, None),
            P(None, "chan", None),
            P("chan", SPACE, None),
            P(SPACE, None),
            P(SPACE, None),
        ),
        out_specs=(P("chan", SPACE, None), P("chan", SPACE, None), P(None, "chan", None)),
        check_vma=False,
    )
```
